32 devices in a mesh: face: 4 (over y, x), tile: 8 (over z, core).
Axes of the slice: x: 2, y: 2, z: 4, core: 2. Of those that a mesh axis runs over, the one named last changes fastest.
Arguments:
- fields: bfloat16 [4, 64, 128, 256], P('face', 'tile'), may hold values from -6 to 6
- cotangent: bfloat16 [4, 64, 128, 256], P('face', 'tile'), may hold values from -6 to 6
- edge_match: int32 [4, 2, 3], replicated, may hold values from 0 to 3, as said below
- depth_kernel: bfloat16 [7, 7, 256], replicated, may hold values from -0.875 to 0.875
- depth_bias: float32 [256], replicated, may hold values from -3 to 3
- norm_gain: float32 [256], replicated, may hold values from 0.5 to 1.5
- norm_bias: float32 [256], replicated, may hold values from -3 to 3
- expand_weight: bfloat16 [256, 1024], replicated, may hold values from -0.375 to 0.375
- expand_bias: float32 [1024], replicated, may hold values from -3 to 3
- reduce_weight: bfloat16 [1024, 256], replicated, may hold values from -0.1875 to 0.1875
- reduce_bias: float32 [256], replicated, may hold values from -3 to 3
- layer_scale: float32 [256], replicated, may hold values from 0.5 to 1.5
Outputs:
- result: bfloat16 [4, 64, 128, 256], P('face', 'tile')
- grad_fields: bfloat16 [4, 64, 128, 256], P('face', 'tile')
- grad_kernel: float32 [7, 7, 256], replicated
- grad_expand: float32 [256, 1024], replicated
- grad_reduce: float32 [1024, 256], replicated
- grad_expand_bias: float32 [1024], replicated
- grad_vectors: float32 [5, 256], replicated
The draws below stay inside these ranges and needn't reach their ends.
Inputs may be any that keep to these rules, and one draw needn't show every extreme that they name: edge_match[f, s] = (g, s2, r): side s of strip f is glued to side s2 of strip g, rows reversed where r is 1; the gluing is symmetric; one side of strip f is glued to strip f XOR 1, the other to strip (f + 2) mod 4; at least one glued pair has reversed rows and at least one has not.
All inputs are finite; a program needn't handle non-finite values.
Results may differ from the reference program's by a relative error of at most 0.0067.
Values may be sent and summed in bfloat16 or wider, within the bound.
No kernel may reach another device: no remote copies, remote signals or barrier semaphores. Data moves between devices by JAX's collectives and lax.ppermute only.
A program may use at most 64 MiB of HBM per device.

```python
import math
import jax
import jax.numpy as jnp
from jax import lax

C = 256
HID = 1024
K = 7
FW = 128
FACES = 4
ROWS = 64
CELLS = 32768


def draw_edge_match(key, part):
    faces = jnp.arange(FACES, dtype=jnp.int32)
    first_side = jax.random.randint(jax.random.fold_in(key, 3), (FACES,), 0, 2).astype(jnp.int32)
    pair_flags = jax.random.randint(jax.random.fold_in(key, 5), (FACES,), 0, 2).astype(jnp.int32)
    forced_on = jax.random.randint(jax.random.fold_in(key, 7), (), 0, FACES).astype(jnp.int32)
    forced_off = (forced_on + 1 + jax.random.randint(jax.random.fold_in(key, 9), (), 0, FACES - 1).astype(jnp.int32)) % FACES
    pair_flags = jnp.where(faces == forced_on, 1, jnp.where(faces == forced_off, 0, pair_flags)).astype(jnp.int32)
    half_count = FACES // 2
    across = (faces + half_count) % FACES
    beside = jnp.bitwise_xor(faces, 1)
    across_row = jnp.stack([across, first_side[across], pair_flags[jnp.minimum(faces, across)]], axis=1)
    beside_row = jnp.stack([beside, 1 - first_side[beside], pair_flags[half_count + jnp.minimum(faces, beside) // 2]], axis=1)
    side_zero = jnp.where((first_side == 0)[:, None], across_row, beside_row)
    side_one = jnp.where((first_side == 1)[:, None], across_row, beside_row)
    return jnp.stack([side_zero, side_one], axis=1).astype(jnp.int32)


def block_scale(stream_key, shape, pieces, smallest, high):
    def one(dim, blocks):
        steps = jax.random.uniform(jax.random.fold_in(jax.random.fold_in(stream_key, 6), dim), (blocks,), jnp.float32, smallest / len(pieces), high / len(pieces))
        return jnp.repeat(jnp.exp(steps), shape[dim] // blocks).reshape((-1,) + (1,) * (len(shape) - dim - 1))

    gain = one(*pieces[0])
    for cut in pieces[1:]:
        gain = gain * one(*cut)
    return gain


def noise(key, dims, scale, bound, pieces=(), kind=jnp.bfloat16):
    level = block_scale(key, dims, pieces, -0.22, 0.18) if pieces else 1.0
    values = jax.random.normal(key, dims, jnp.float32) * scale * level
    return jnp.minimum(jnp.maximum(values, -bound), bound).astype(kind)


def setup_inputs(seed: int = 0) -> dict:
    key_of = jax.random.split(jax.random.key(seed), 13)
    return {
        "fields": noise(key_of[0], (FACES, ROWS, FW, C), 1.0, 6.0, ((0, 4), (1, 8))),
        "cotangent": noise(key_of[1], (FACES, ROWS, FW, C), 1.0, 6.0, ((0, 4), (1, 8))),
        "edge_match": draw_edge_match(jax.random.fold_in(key_of[12], 71), 0),
        "depth_kernel": noise(key_of[3], (K, K, C), (K * K) ** -0.5, 0.875),
        "depth_bias": noise(key_of[4], (C,), 0.5, 3.0, (), jnp.float32),
        "norm_gain": jnp.clip(jax.random.uniform(key_of[5], (C,), jnp.float32, 0.5, 1.5), 0.5, 1.5),
        "norm_bias": noise(key_of[6], (C,), 0.5, 3.0, (), jnp.float32),
        "expand_weight": noise(key_of[7], (C, HID), C ** -0.5, 0.375),
        "expand_bias": noise(key_of[8], (HID,), 0.5, 3.0, (), jnp.float32),
        "reduce_weight": noise(key_of[9], (HID, C), HID ** -0.5, 0.1875),
        "reduce_bias": noise(key_of[10], (C,), 0.5, 3.0, (), jnp.float32),
        "layer_scale": jnp.clip(jax.random.uniform(key_of[11], (C,), jnp.float32, 0.5, 1.5), 0.5, 1.5),
    }


EPSILON = 1e-06
ROOT_COEF = 0.7978845608028654
CUBIC_COEF = 0.044715

def gelu_pair(preact):
    argument = ROOT_COEF * (preact + CUBIC_COEF * preact * preact * preact)
    tanhed = jnp.tanh(argument)
    gelu_value = 0.5 * preact * (1.0 + tanhed)
    gelu_slope = 0.5 * (1.0 + tanhed) + 0.5 * preact * (1.0 - tanhed * tanhed) * ROOT_COEF * (1.0 + 3.0 * CUBIC_COEF * preact * preact)
    return (gelu_value, gelu_slope)

def contract_rows(left_side, right_side):
    return lax.dot_general(left_side, right_side, (((0,), (0,)), ((), ())), preferred_element_type=jnp.float32)

def contract_cols(left_side, right_side):
    return lax.dot_general(left_side, right_side, (((1,), (1,)), ((), ())), preferred_element_type=jnp.float32)

def block_pass(padded, face_grid, face_cot, kernel, depth_bias, norm_gain, norm_bias, expand_weight, expand_bias, reduce_weight, reduce_bias, layer_scale):
    row_count, col_count, channels = face_grid.shape
    kernel_size = kernel.shape[0]
    convolved = jnp.zeros((row_count, col_count, channels), jnp.float32) + depth_bias
    for row_off in range(kernel_size):
        for col_off in range(kernel_size):
            convolved = convolved + kernel[row_off, col_off] * padded[row_off:row_off + row_count, col_off:col_off + col_count]
    average = lax.optimization_barrier(jnp.mean(convolved, axis=-1, keepdims=True))
    centred = convolved - average
    inverse = lax.rsqrt(lax.optimization_barrier(jnp.mean(centred * centred, axis=-1, keepdims=True)) + EPSILON)
    standard = centred * inverse
    normed = (standard * norm_gain + norm_bias).astype(jnp.bfloat16).reshape(row_count * col_count, channels)
    preact = jnp.dot(normed, expand_weight, preferred_element_type=jnp.float32) + expand_bias
    gelu_value, gelu_slope = gelu_pair(preact)
    activated = gelu_value.astype(jnp.bfloat16)
    branch = jnp.dot(activated, reduce_weight, preferred_element_type=jnp.float32) + reduce_bias
    residual = face_grid.reshape(row_count * col_count, channels).astype(jnp.float32)
    result = (residual + layer_scale * branch).astype(jnp.bfloat16).reshape(row_count, col_count, channels)
    upstream = face_cot.reshape(row_count * col_count, channels).astype(jnp.float32)
    grad_branch = (upstream * layer_scale).astype(jnp.bfloat16)
    grad_pre = (contract_cols(grad_branch, reduce_weight) * gelu_slope).astype(jnp.bfloat16)
    grad_normed = contract_cols(grad_pre, expand_weight).reshape(row_count, col_count, channels)
    scaled = grad_normed * norm_gain
    grad_conv = (scaled - lax.optimization_barrier(jnp.mean(scaled, axis=-1, keepdims=True)) - standard * lax.optimization_barrier(jnp.mean(scaled * standard, axis=-1, keepdims=True))) * inverse
    dz_padded = jnp.pad(grad_conv, ((6, 6), (6, 6), (0, 0)))
    grad_padded = jnp.zeros((row_count + 6, col_count + 6, channels), jnp.float32)
    kernel_terms = []
    for row_off in range(kernel_size):
        for col_off in range(kernel_size):
            grad_padded = grad_padded + kernel[row_off, col_off] * dz_padded[6 - row_off:12 - row_off + row_count, 6 - col_off:12 - col_off + col_count]
            kernel_terms.append(lax.optimization_barrier(jnp.sum(grad_conv * padded[row_off:row_off + row_count, col_off:col_off + col_count], axis=(0, 1))))
    grad_kernel = jnp.stack(kernel_terms).reshape(kernel_size, kernel_size, channels)
    grad_expand = contract_rows(normed, grad_pre)
    grad_reduce = contract_rows(activated, grad_branch)
    grad_expand_bias = lax.optimization_barrier(jnp.sum(grad_pre.astype(jnp.float32), axis=0))
    vectors = jnp.stack([lax.optimization_barrier(jnp.sum(grad_conv, axis=(0, 1))), lax.optimization_barrier(jnp.sum(grad_normed * standard, axis=(0, 1))), lax.optimization_barrier(jnp.sum(grad_normed, axis=(0, 1))), lax.optimization_barrier(jnp.sum(upstream, axis=0)) * layer_scale, lax.optimization_barrier(jnp.sum(upstream * branch, axis=0))])
    return (result, grad_padded, (grad_kernel, grad_expand, grad_reduce, grad_expand_bias, vectors))

def edge_depths(grids):
    west_side = grids[:, :, 0:3]
    east_side = jnp.flip(grids[:, :, FW - 3:], 2)
    return jnp.stack([west_side, east_side], axis=1)

def glue(depths, edge_match):
    chosen = depths[edge_match[:, :, 0], edge_match[:, :, 1]]
    reverse_flag = edge_match[:, :, 2][:, :, None, None, None]
    return jnp.where(reverse_flag == 1, jnp.flip(chosen, 2), chosen)

def reference(fields, cotangent, edge_match, depth_kernel, depth_bias, norm_gain, norm_bias, expand_weight, expand_bias, reduce_weight, reduce_bias, layer_scale):
    ghost_all = glue(edge_depths(fields), edge_match)
    kernel = depth_kernel.astype(jnp.float32)

    def face_step(totals, face_item):
        face_grid, face_cot, ghosts = face_item
        widened = jnp.concatenate([jnp.flip(ghosts[0], 1), face_grid, ghosts[1]], axis=1)
        padded = jnp.pad(widened, ((3, 3), (0, 0), (0, 0))).astype(jnp.float32)
        result, grad_padded, terms = block_pass(padded, face_grid, face_cot, kernel, depth_bias, norm_gain, norm_bias, expand_weight, expand_bias, reduce_weight, reduce_bias, layer_scale)
        interior = face_cot.astype(jnp.float32) + grad_padded[3:ROWS + 3, 3:FW + 3]
        ghost_grads = jnp.stack([jnp.flip(grad_padded[3:ROWS + 3, 0:3], 1), grad_padded[3:ROWS + 3, FW + 3:FW + 6]])
        totals = tuple((total + term for total, term in zip(totals, terms)))
        return (totals, (result, interior, ghost_grads))
    zero_totals = (jnp.zeros((K, K, C), jnp.float32), jnp.zeros((C, HID), jnp.float32), jnp.zeros((HID, C), jnp.float32), jnp.zeros((HID,), jnp.float32), jnp.zeros((5, C), jnp.float32))
    totals, (results, interior, ghost_grads) = lax.scan(face_step, zero_totals, (fields, cotangent, ghost_all))
    returned = glue(ghost_grads, edge_match)
    interior = interior.at[:, :, 0:3].add(returned[:, 0])
    interior = interior.at[:, :, FW - 3:].add(jnp.flip(returned[:, 1], 2))
    factor = 1.0 / math.sqrt(CELLS)
    return (results, interior.astype(jnp.bfloat16), totals[0] * factor, totals[1] * factor, totals[2] * factor, totals[3] * factor, totals[4] * factor)
```

```python
import math

import jax
import jax.numpy as jnp
from jax import lax
from jax.experimental import pallas as pl
from jax.experimental.pallas import tpu as pltpu
from jax.sharding import PartitionSpec as P

EPSILON = 1e-06
ROOT_COEF = 0.7978845608028654
CUBIC_COEF = 0.044715
LANES = 128
SUB = 8
LEAD = 8
F32 = jnp.float32
BF16 = jnp.bfloat16


def swapped(x, axis, mask):
    return lax.ppermute(x, axis, [(i, i ^ mask) for i in range(lax.axis_size(axis))])


def dot(a, b, dims):
    return lax.dot_general(a, b, (dims, ((), ())), preferred_element_type=F32)


def whole(n):
    return [pl.BlockSpec(memory_space=pltpu.VMEM)] * n


def call(body, outs, scratch, flops, *args):
    return pl.pallas_call(
        body,
        out_shape=outs,
        in_specs=whole(len(args)),
        out_specs=whole(len(outs)),
        scratch_shapes=scratch,
        compiler_params=pltpu.CompilerParams(vmem_limit_bytes=40 * 1024 * 1024),
        cost_estimate=pl.CostEstimate(flops=flops, bytes_accessed=4 << 20, transcendentals=0),
    )(*args)


def forward_kernel(
    band, up, down, west, east, cot, taps, chan, bias1, w1, w2, core,
    result, pad, grad, mine, other, vecs, bias_out,
    conv, normed, act, pre, gbr, tmp,
):
    rows, cols, channels = band.shape
    halves = channels // LANES
    pitch = cols + 2 * LEAD
    ext = rows + 6
    groups = cols // SUB
    hidden = w1.shape[1]
    cells = rows * cols

    for h in range(halves):
        lane = slice(h * LANES, (h + 1) * LANES)
        for i in range(ext):
            at = (h * ext + i) * pitch
            src = up[i] if i < 3 else (band[i - 3] if i < rows + 3 else down[i - rows - 3])
            pad[at : at + LEAD, :] = west[i][:, lane].astype(F32)
            pad[at + LEAD : at + LEAD + cols, :] = src[:, lane].astype(F32)
            pad[at + LEAD + cols : at + pitch, :] = east[i][:, lane].astype(F32)
        for r in range(rows):
            at = (h * rows + r) * pitch
            grad[at : at + LEAD, :] = jnp.zeros((LEAD, LANES), F32)
            grad[at + LEAD + cols : at + pitch, :] = jnp.zeros((LEAD, LANES), F32)

    for h in range(halves):
        first = jnp.broadcast_to(chan[0:1, h * LANES : (h + 1) * LANES], (SUB, LANES))

        def conv_row(r, carry, h=h, first=first):
            acc = [first] * groups
            for a in range(7):
                base = (h * ext + r + a) * pitch + LEAD - 3
                tap = [taps[h, a * 7 + b] for b in range(7)]
                for jj in range(groups + 6):
                    x = pad[pl.ds(base + jj, SUB, stride=groups), :]
                    for b in range(7):
                        j = jj - b
                        if 0 <= j < groups:
                            acc[j] = acc[j] + tap[b] * x
            for j in range(groups):
                conv[pl.ds((h * rows + r) * cols + j, SUB, stride=groups), :] = acc[j]
            return carry

        lax.fori_loop(0, rows, conv_row, 0)

    step = 2 * cols
    gain = chan[1:2, :]
    shift = chan[2:3, :]
    bias2 = chan[3:4, :]
    scale = chan[4:5, :]
    tiles = hidden // 256

    def chunk(m, carry):
        s_conv, s_gain, s_norm, s_cot, s_scale = carry
        at = pl.multiple_of(m * step, step)
        x = jnp.concatenate(
            [conv[pl.ds(h * cells + at, step), :] for h in range(halves)], axis=1
        )
        centred = x - jnp.mean(x, axis=-1, keepdims=True)
        inverse = lax.rsqrt(jnp.mean(centred * centred, axis=-1, keepdims=True) + EPSILON)
        standard = centred * inverse
        lane_in = (standard * gain + shift).astype(BF16)
        normed[pl.ds(at, step), :] = lane_in
        tmp[...] = standard
        upstream = cot[pl.ds(2 * m, 2)].reshape(step, channels).astype(F32)
        g_branch = (upstream * scale).astype(BF16)
        gbr[pl.ds(at, step), :] = g_branch
        for n in range(tiles):
            hid = slice(n * 256, (n + 1) * 256)
            v = dot(lane_in, w1[:, hid], ((1,), (0,))) + bias1[:, hid]
            v2 = v * v
            half = 0.5 + 0.5 * jnp.tanh(v * (ROOT_COEF + ROOT_COEF * CUBIC_COEF * v2))
            act[pl.ds(at, step), hid] = (v * half).astype(BF16)
            slope = half * (
                1.0 + (1.0 - half) * (v * (2 * ROOT_COEF + 6 * ROOT_COEF * CUBIC_COEF * v2))
            )
            d_act = dot(g_branch, w2[hid, :], ((1,), (1,)))
            g_pre = (d_act * slope).astype(BF16)
            pre[pl.ds(at, step), hid] = g_pre
            bias_out[:, hid] += jnp.sum(g_pre.astype(F32), axis=0, keepdims=True)
        branch = dot(act[pl.ds(at, step), :], w2[...], ((1,), (0,))) + bias2
        residual = band[pl.ds(2 * m, 2)].reshape(step, channels).astype(F32)
        result[pl.ds(2 * m, 2)] = (residual + scale * branch).astype(BF16).reshape(2, cols, channels)
        s_cot = s_cot + jnp.sum(upstream, axis=0, keepdims=True)
        s_scale = s_scale + jnp.sum(upstream * branch, axis=0, keepdims=True)
        g_norm = dot(pre[pl.ds(at, step), :], w1[...], ((1,), (1,)))
        standard = tmp[...]
        u = g_norm * gain
        g_conv = (
            u
            - jnp.mean(u, axis=-1, keepdims=True)
            - standard * jnp.mean(u * standard, axis=-1, keepdims=True)
        ) * inverse
        for h in range(halves):
            for k in range(2):
                dst = (h * rows + 2 * m + k) * pitch + LEAD
                grad[pl.ds(pl.multiple_of(dst, 8), cols), :] = g_conv[
                    k * cols : (k + 1) * cols, h * LANES : (h + 1) * LANES
                ]
        s_conv = s_conv + jnp.sum(g_conv, axis=0, keepdims=True)
        s_gain = s_gain + jnp.sum(g_norm * standard, axis=0, keepdims=True)
        s_norm = s_norm + jnp.sum(g_norm, axis=0, keepdims=True)
        return (s_conv, s_gain, s_norm, s_cot, s_scale)

    bias_out[...] = jnp.zeros_like(bias_out)
    zero = jnp.zeros((1, channels), F32)
    sums = lax.fori_loop(0, rows // 2, chunk, (zero,) * 5)
    sums = (sums[0], sums[1], sums[2], sums[3] * scale, sums[4])
    vecs[...] = jnp.concatenate(list(sums) + [zero] * 3, axis=0)

    even = core[0, 0] == 0
    for n in range(tiles):
        hid = slice(n * 256, (n + 1) * 256)
        g_expand = dot(normed[...], pre[:, hid], ((0,), (0,)))
        g_reduce = dot(act[:, hid], gbr[...], ((0,), (0,)))
        mine[n] = jnp.where(even, g_expand, g_reduce)
        other[n] = jnp.where(even, g_reduce, g_expand).astype(BF16)


def spread_kernel(grad, taps, out):
    halves = taps.shape[0]
    pitch = out.shape[2]
    ext = out.shape[1]
    rows = ext - 6
    cols = pitch - 2 * LEAD
    groups = cols // SUB + 1
    out[...] = jnp.zeros_like(out)
    flat = out.reshape(halves * ext * pitch, LANES)
    for h in range(halves):

        def row(r, carry, h=h):
            src = (h * rows + r) * pitch + LEAD
            for a in range(7):
                dst = (h * ext + r + a) * pitch + LEAD - 3
                tap = [taps[h, a * 7 + b] for b in range(7)]
                acc = [flat[pl.ds(dst + j, SUB, stride=groups), :] for j in range(groups)]
                for jj in range(-6, groups):
                    x = grad[pl.ds(src + jj, SUB, stride=groups), :]
                    for b in range(7):
                        j = jj + b
                        if 0 <= j < groups:
                            acc[j] = acc[j] + tap[b] * x
                for j in range(groups):
                    flat[pl.ds(dst + j, SUB, stride=groups), :] = acc[j]
            return carry

        lax.fori_loop(0, rows, row, 0)


def taps_kernel(grad, pad, out):
    pitch = 128 + 2 * LEAD
    halves = out.shape[0]
    rows = grad.shape[0] // (halves * pitch)
    ext = rows + 6
    cols = pitch - 2 * LEAD
    groups = cols // SUB
    for h in range(halves):

        def one(a, carry, h=h):
            acc = [jnp.zeros((SUB, LANES), F32)] * 7
            for r in range(rows):
                src = (h * rows + r) * pitch + LEAD
                base = (h * ext + r + a) * pitch + LEAD - 3
                g = [grad[pl.ds(src + j, SUB, stride=groups), :] for j in range(groups)]
                for jj in range(groups + 6):
                    x = pad[pl.ds(base + jj, SUB, stride=groups), :]
                    for b in range(7):
                        j = jj - b
                        if 0 <= j < groups:
                            acc[b] = acc[b] + g[j] * x
            for b in range(7):
                out[h, pl.ds(a * 7 + b, 1), :] = jnp.sum(acc[b], axis=0, keepdims=True)
            return carry

        lax.fori_loop(0, 7, one, 0)


def partner_swap(by_side, edge_match):
    faces = lax.axis_size("face")
    tiles = lax.axis_size("tile")
    own = lax.dynamic_index_in_dim(edge_match, lax.axis_index("face"), 0, keepdims=False)
    face = lax.axis_index("face")
    near_side = jnp.where(own[0, 0] == face ^ 1, 0, 1)
    got = []
    for which, mask in ((0, 1), (1, faces // 2)):
        side = near_side if which == 0 else 1 - near_side
        reverse = own[side, 2] == 1
        sent = lax.dynamic_index_in_dim(by_side, side, 0, keepdims=False)
        pairs = [
            (f * tiles + t, (f ^ mask) * tiles + t) for f in range(faces) for t in range(tiles)
        ]
        turned = [
            (f * tiles + t, (f ^ mask) * tiles + tiles - 1 - t)
            for f in range(faces)
            for t in range(tiles)
        ]
        plain = lax.ppermute(sent, ("face", "tile"), pairs)
        flipped = lax.ppermute(sent, ("face", "tile"), turned)
        got.append(jnp.where(reverse, jnp.flip(flipped, 0), plain))
    first, second = got
    return jnp.where(near_side == 0, first, second), jnp.where(near_side == 0, second, first)


def row_exchange(to_up, to_down):
    count = lax.axis_size("tile")
    from_up = lax.ppermute(to_down, "tile", [(i, i + 1) for i in range(count - 1)])
    from_down = lax.ppermute(to_up, "tile", [(i + 1, i) for i in range(count - 1)])
    return from_up, from_down


def bit_of(axis, mask):
    return (lax.axis_index(axis) & mask) // mask


def face_and_tile_steps():
    face = [("face", 1 << k) for k in range(lax.axis_size("face").bit_length() - 1)]
    tile = [("tile", 1 << k) for k in range(1, lax.axis_size("tile").bit_length() - 1)]
    return face + tile, face[1::-1] + face[2:] + tile


def halving(x, step):
    axis, mask = step
    bit = bit_of(axis, mask)
    pair = x.reshape((2, x.shape[0] // 2) + x.shape[1:])
    kept = lax.dynamic_index_in_dim(pair, bit, 0, keepdims=False)
    sent = lax.dynamic_index_in_dim(pair, 1 - bit, 0, keepdims=False).astype(BF16)
    return kept + swapped(sent, axis, mask).astype(F32)


def doubling(x, step):
    axis, mask = step
    bit = bit_of(axis, mask)
    got = swapped(x, axis, mask)
    return jnp.where(bit == 0, jnp.concatenate([x, got], 0), jnp.concatenate([got, x], 0))


def shards(
    fields,
    cotangent,
    edge_match,
    depth_kernel,
    depth_bias,
    norm_gain,
    norm_bias,
    expand_weight,
    expand_bias,
    reduce_weight,
    reduce_bias,
    layer_scale,
):
    band = fields[0]
    cot = cotangent[0]
    rows, cols, channels = band.shape
    halves = channels // LANES
    hidden = expand_weight.shape[1]
    pitch = cols + 2 * LEAD
    ext = rows + 6
    cells = rows * cols

    up, down = row_exchange(band[0:3], band[rows - 3 :])
    tall_west = jnp.concatenate([up[:, 0:3], band[:, 0:3], down[:, 0:3]], 0)
    tall_east = jnp.concatenate(
        [up[:, cols - 3 :], band[:, cols - 3 :], down[:, cols - 3 :]], 0
    )
    west, east = partner_swap(jnp.stack([tall_west, jnp.flip(tall_east, 1)]), edge_match)
    west = jnp.pad(jnp.flip(west, 1), ((0, 0), (LEAD - 3, 0), (0, 0)))
    east = jnp.pad(east, ((0, 0), (0, LEAD - 3), (0, 0)))

    taps = depth_kernel.astype(F32).reshape(49, halves, 1, LANES).transpose(1, 0, 2, 3)
    taps = jnp.broadcast_to(taps, (halves, 49, SUB, LANES))
    zero = jnp.zeros((3, channels), F32)
    chan = jnp.concatenate(
        [jnp.stack([depth_bias, norm_gain, norm_bias, reduce_bias, layer_scale]), zero], 0
    )
    core = jnp.full((1, LANES), lax.axis_index("tile") & 1, jnp.int32)

    shape = jax.ShapeDtypeStruct
    result, pad, grad, mine, other, vecs, bias_out = call(
        forward_kernel,
        [
            shape(band.shape, BF16),
            shape((halves * ext * pitch, LANES), F32),
            shape((halves * rows * pitch, LANES), F32),
            shape((hidden // 256, 256, 256), F32),
            shape((hidden // 256, 256, 256), BF16),
            shape((8, channels), F32),
            shape((1, hidden), F32),
        ],
        [
            pltpu.VMEM((halves * cells, LANES), F32),
            pltpu.VMEM((cells, channels), BF16),
            pltpu.VMEM((cells, hidden), BF16),
            pltpu.VMEM((cells, hidden), BF16),
            pltpu.VMEM((cells, channels), BF16),
            pltpu.VMEM((2 * cols, channels), F32),
        ],
        3_000_000_000,
        band, up, down, west, east, cot, taps, chan,
        expand_bias.reshape(1, hidden), expand_weight, reduce_weight, core,
    )

    total = mine + swapped(other, "tile", 1).astype(F32)
    total = total.reshape(hidden, 256)
    order_a, order_b = face_and_tile_steps()
    part_a, part_b = total[: hidden // 2], total[hidden // 2 :]
    for step_a, step_b in zip(order_a, order_b):
        part_a, part_b = halving(part_a, step_a), halving(part_b, step_b)

    (wide,) = call(
        spread_kernel, [shape((halves, ext, pitch, LANES), F32)], [], 1_000_000_000, grad, taps
    )
    (g_taps,) = call(taps_kernel, [shape((halves, 49, LANES), F32)], [], 1_000_000_000, grad, pad)

    small = jnp.concatenate(
        [
            g_taps.transpose(1, 0, 2).reshape(49, channels),
            bias_out.reshape(hidden // channels, channels),
            vecs[0:5],
            jnp.zeros((64 - 54 - hidden // channels, channels), F32),
        ],
        0,
    )
    part_a, part_b = part_a.astype(BF16), part_b.astype(BF16)
    for step_a, step_b in zip(order_a[::-1], order_b[::-1]):
        part_a, part_b = doubling(part_a, step_a), doubling(part_b, step_b)
        small = small + swapped(small, *step_a)
    total = jnp.concatenate([part_a, part_b], 0)
    small = small + swapped(small, "tile", 1)
    peer = swapped(total, "tile", 1)
    even = (lax.axis_index("tile") & 1) == 0
    factor = 1.0 / math.sqrt(lax.axis_size("face") * lax.axis_size("tile") * cells)
    g_expand = jnp.where(even, total, peer).astype(F32) * factor
    g_expand = g_expand.reshape(hidden // 256, 256, 256).transpose(1, 0, 2).reshape(channels, hidden)
    g_reduce = jnp.where(even, peer, total).astype(F32) * factor
    small = small * factor

    rim = wide.astype(BF16)
    arrived_up, arrived_down = row_exchange(rim[:, 0:3], rim[:, rows + 3 :])
    middle = wide[:, 3 : rows + 3]
    middle = middle.at[:, 0:3].add(arrived_up.astype(F32))
    middle = middle.at[:, rows - 3 :].add(arrived_down.astype(F32))
    ghost_west = jnp.flip(middle[:, :, LEAD - 3 : LEAD], 2)
    ghost_east = middle[:, :, LEAD + cols : LEAD + cols + 3]
    ghosts = jnp.stack([ghost_west, ghost_east]).astype(BF16).transpose(0, 2, 3, 1, 4)
    back_west, back_east = partner_swap(ghosts.reshape(2, rows, 3, channels), edge_match)
    inner = middle[:, :, LEAD : LEAD + cols].transpose(1, 2, 0, 3).reshape(rows, cols, channels)
    inner = inner.at[:, 0:3].add(back_west.astype(F32))
    inner = inner.at[:, cols - 3 :].add(jnp.flip(back_east, 1).astype(F32))
    grad_fields = (cot.astype(F32) + inner).astype(BF16)

    n_bias = hidden // channels
    return (
        result[None],
        grad_fields[None],
        small[0:49].reshape(7, 7, channels),
        g_expand,
        g_reduce,
        small[49 : 49 + n_bias].reshape(hidden),
        small[49 + n_bias : 54 + n_bias],
    )


def solution(mesh):
    return jax.shard_map(
        shards,
        mesh=mesh,
        in_specs=(P("face", "tile"), P("face", "tile")) + (P(),) * 10,
        out_specs=(P("face", "tile"), P("face", "tile")) + (P(),) * 5,
        check_vma=False,
    )
```

```python
import math

import jax
import jax.numpy as jnp
from jax import lax
from jax.experimental import pallas as pl
from jax.experimental.pallas import tpu as pltpu
from jax.sharding import PartitionSpec as P

EPSILON = 1e-06
ROOT_COEF = 0.7978845608028654
CUBIC_COEF = 0.044715
LANES = 128
SUB = 8
LEAD = 8
SMALL = 64
F32 = jnp.float32
BF16 = jnp.bfloat16


def dot(a, b, dims):
    return lax.dot_general(a, b, (dims, ((), ())), preferred_element_type=F32)


def call(body, outs, scratch, flops, args, smem=0, after=(), limit=4, left=()):
    vmem = pl.BlockSpec(memory_space=pltpu.VMEM)
    scalar = pl.BlockSpec(memory_space=pltpu.SMEM)
    anywhere = pl.BlockSpec(memory_space=pl.ANY)
    outside = pl.BlockSpec(memory_space=pltpu.HBM)
    count = len(args)

    def run(*refs):
        body(*refs[:count], *refs[count + len(after) :])

    return pl.pallas_call(
        run,
        out_shape=outs,
        in_specs=[vmem] * (count - smem) + [scalar] * smem + [anywhere] * len(after),
        out_specs=[outside if i in left else vmem for i in range(len(outs))],
        scratch_shapes=scratch,
        compiler_params=pltpu.CompilerParams(vmem_limit_bytes=limit * 1024 * 1024),
        cost_estimate=pl.CostEstimate(flops=flops, bytes_accessed=1 << 20, transcendentals=0),
    )(*args, *after)


def kept(x):
    return pltpu.with_memory_space_constraint(x, pltpu.VMEM)


def strided(ref, start, groups):
    return ref[pl.ds(start, SUB, stride=groups), :]


def gluing(match):
    face = lax.axis_index("face")
    near = jnp.where(match[face, 0, 0] == face ^ 1, 0, 1)
    return near, match[face, near, 2], match[face, 1 - near, 2]


def pack_columns(tile, count, near, held, outs):
    vals = {}
    for side in range(2):
        for h in range(2):
            held[...] = jnp.zeros_like(held)
            for i in range(count):
                t = tile(side, h, i)
                held[0, i * SUB : (i + 1) * SUB, :] = t
                held[1, (count - 1 - i) * SUB : (count - i) * SUB, :] = t
            for v in range(2):
                for d in range(3):
                    vals[side, h, v, d] = held[v, pl.ds(tile.column(side, d), 16, stride=SUB), :]
    first = near == 0
    for h in range(2):
        lane = slice(h * LANES, (h + 1) * LANES)
        for v in range(2):
            for d in range(3):
                west, east = vals[0, h, v, d], vals[1, h, v, d]
                at = slice(d * 16, d * 16 + 16)
                outs[v][at, lane] = jnp.where(first, west, east).astype(BF16)
                outs[2 + v][at, lane] = jnp.where(first, east, west).astype(BF16)


def unpack_columns(near, turn_near, turn_far, got):
    first = near == 0

    def value(side, h, d):
        lane = slice(h * LANES, (h + 1) * LANES)
        parts = [g[d * 16 : d * 16 + 16, lane].astype(F32) for g in got]
        one = jnp.where(turn_near == 1, parts[1], parts[0])
        two = jnp.where(turn_far == 1, parts[3], parts[2])
        return jnp.where(first, one, two) if side == 0 else jnp.where(first, two, one)

    return value


def ends_kernel(band, within, across, columns):
    rows, cols, _ = band.shape
    even = (lax.axis_index("tile") & 1) == 0
    for k in range(3):
        top, bottom = band[k], band[rows - 3 + k]
        within[k] = jnp.where(even, bottom, top)
        across[k] = jnp.where(even, top, bottom)
    for r in range(rows):
        columns[r, 0:16, :] = band[r, 0:16, :]
        columns[r, 16:32, :] = band[r, cols - 16 : cols, :]


def edges_kernel(columns, within, across, match, *refs):
    outs, held = refs[:4], refs[4]
    up, down = above_below(within, across)
    rows, _, _ = columns.shape
    _, cols, _ = within.shape
    near, _, _ = gluing(match)

    def tile(side, h, i):
        lane = slice(h * LANES, (h + 1) * LANES)
        at = slice(0, 16) if side == 0 else slice(cols - 16, cols)
        if i < 3:
            v = up(i, at, lane)
        elif i < rows + 3:
            v = columns[i - 3, slice(0, 16) if side == 0 else slice(16, 32), lane]
        else:
            v = down(i - rows - 3, at, lane)
        return v.astype(F32)[0:SUB] if side == 0 else v.astype(F32)[SUB:16]

    tile.column = lambda side, d: d if side == 0 else SUB - 1 - d
    pack_columns(tile, rows + 6, near, held, outs)


def fill_pad(pad, halves, ext, wide, cols, source, which):
    for h in range(halves):
        lane = slice(h * LANES, (h + 1) * LANES)
        for i in which:
            at = (h * ext + i) * wide
            pad[at : at + LEAD, :] = jnp.zeros((LEAD, LANES), F32)
            pad[at + LEAD : at + LEAD + cols, :] = source(i, lane).astype(F32)
            pad[at + LEAD + cols : at + wide, :] = jnp.zeros((LEAD + SUB, LANES), F32)


def own_rows_kernel(band, kernel, bias, conv, taps, pad):
    for h in range(2):
        lane = slice(h * LANES, (h + 1) * LANES)
        for a in range(7):
            row = kernel[a].astype(F32)
            for b in range(7):
                taps[h, a * 7 + b] = jnp.broadcast_to(row[b : b + 1, lane], (SUB, LANES))
        taps[h, 49] = jnp.broadcast_to(bias[:, lane], (SUB, LANES))
    rows, cols, channels = band.shape
    halves = channels // LANES
    pitch = cols + 2 * LEAD
    wide = pitch + SUB
    ext = rows + 6
    groups = cols // SUB + 1
    cpitch = groups * SUB
    fill_pad(pad, halves, ext, wide, cols, lambda i, lane: band[i - 3, :, lane], range(3, rows + 3))

    def half(h, carry):
        for r in range(rows):
            acc = [taps[h, 49]] * groups
            for a in range(7):
                if not 3 <= r + a < rows + 3:
                    continue
                base = (h * ext + r + a) * wide + LEAD - 3
                tap = [taps[h, a * 7 + b] for b in range(7)]
                for jj in range(groups + 6):
                    x = strided(pad, base + jj, groups)
                    for b in range(7):
                        if 0 <= jj - b < groups:
                            acc[jj - b] = acc[jj - b] + tap[b] * x
            for j in range(groups):
                conv[pl.ds((h * rows + r) * cpitch + j, SUB, stride=groups), :] = acc[j]
        return carry

    lax.fori_loop(0, halves, half, 0)


def forward_kernel(
    band, within, across, got0, got1, got2, got3, cot, taps, gain, shift, bias2, scale, bias1, w1, w2, part, match,
    result_out, pad_out, grad_out, mine, other, plain_near, plain_far, rim, vecs, bias_out,
    result, pad, grad, conv, normed, act, pre, gbr, tmp, strip, sems,
):
    rows, cols, channels = band.shape
    halves = channels // LANES
    pitch = cols + 2 * LEAD
    wide = pitch + SUB
    ext = rows + 6
    groups = cols // SUB + 1
    cpitch = groups * SUB
    hidden = w1.shape[1]

    near, turn_near, turn_far = gluing(match)
    arrived = unpack_columns(near, turn_near, turn_far, (got0, got1, got2, got3))

    up, down = above_below(within, across)

    def source(i, lane):
        if i < 3:
            return up(i, slice(None), lane)
        return band[i - 3, :, lane] if i < rows + 3 else down(i - rows - 3, slice(None), lane)

    fill_pad(pad, halves, ext, wide, cols, source, range(ext))
    for h in range(halves):
        for d in range(3):
            for side in range(2):
                col = LEAD - 1 - d if side == 0 else LEAD + cols + d
                v = arrived(side, h, d)
                at = h * ext * wide + col
                pad[pl.ds(at, SUB, stride=wide), :] = v[0:SUB]
                pad[pl.ds(at + SUB * wide, ext - SUB, stride=wide), :] = v[SUB:ext]
        for r in range(rows):
            at = (h * rows + r) * pitch
            grad[at : at + LEAD, :] = jnp.zeros((LEAD, LANES), F32)
            grad[at + LEAD + cols : at + pitch, :] = jnp.zeros((LEAD, LANES), F32)

    keep_pad = pltpu.make_async_copy(pad, pad_out, sems.at[0])
    keep_pad.start()
    tail = halves * rows * pitch
    grad[tail : tail + SUB, :] = jnp.zeros((SUB, LANES), F32)

    where = lax.broadcasted_iota(jnp.int32, (SUB, LANES), 0)
    at_west, at_east = where == 0, where == SUB - 1
    none = jnp.zeros((SUB, LANES), F32)
    over = cols + 3 - (SUB - 1) * groups

    def complete(h, carry):
        for r in range(rows):
            acc = [strided(part, (h * rows + r) * cpitch + j, groups) for j in range(groups)]
            for a in range(7):
                base = (h * ext + r + a) * wide + LEAD - 3
                tap = [taps[h, a * 7 + b] for b in range(7)]
                if not 3 <= r + a < rows + 3:
                    for jj in range(groups + 6):
                        x = strided(pad, base + jj, groups)
                        for b in range(7):
                            if 0 <= jj - b < groups:
                                acc[jj - b] = acc[jj - b] + tap[b] * x
                    continue
                for d in range(3):
                    x = jnp.where(at_west, strided(pad, base + d, groups), none)
                    for b in range(d + 1):
                        acc[d - b] = acc[d - b] + tap[b] * x
                    x = jnp.where(at_east, strided(pad, base + over + d, groups), none)
                    for b in range(4 + d, 7):
                        acc[over + d - b] = acc[over + d - b] + tap[b] * x
            for j in range(groups):
                conv[pl.ds((h * rows + r) * cpitch + j, SUB, stride=groups), :] = acc[j]
        return carry

    lax.fori_loop(0, halves, complete, 0)

    step = 2 * cols
    gain, shift, bias2, scale = gain[...], shift[...], bias2[...], scale[...]
    tiles = hidden // 256

    def chunk(m, carry):
        s_conv, s_gain, s_norm, s_cot, s_scale = carry
        at = pl.multiple_of(m * step, step)
        x = jnp.concatenate(
            [
                jnp.concatenate(
                    [
                        conv[pl.ds(pl.multiple_of((h * rows + 2 * m + k) * cpitch, 8), cols), :]
                        for k in range(2)
                    ],
                    axis=0,
                )
                for h in range(halves)
            ],
            axis=1,
        )
        centred = x - jnp.mean(x, axis=-1, keepdims=True)
        inverse = lax.rsqrt(jnp.mean(centred * centred, axis=-1, keepdims=True) + EPSILON)
        standard = centred * inverse
        lane_in = (standard * gain + shift).astype(BF16)
        normed[pl.ds(at, step), :] = lane_in
        tmp[...] = standard
        upstream = cot[pl.ds(2 * m, 2)].reshape(step, channels).astype(F32)
        g_branch = (upstream * scale).astype(BF16)
        gbr[pl.ds(at, step), :] = g_branch
        for n in range(tiles):
            hid = slice(n * 256, (n + 1) * 256)
            v = dot(lane_in, w1[:, hid], ((1,), (0,))) + bias1[:, hid]
            v2 = v * v
            half = 0.5 + 0.5 * jnp.tanh(v * (ROOT_COEF + ROOT_COEF * CUBIC_COEF * v2))
            act[pl.ds(at, step), hid] = (v * half).astype(BF16)
            slope = half * (
                1.0 + (1.0 - half) * (v * (2 * ROOT_COEF + 6 * ROOT_COEF * CUBIC_COEF * v2))
            )
            d_act = dot(g_branch, w2[hid, :], ((1,), (1,)))
            g_pre = (d_act * slope).astype(BF16)
            pre[pl.ds(at, step), hid] = g_pre
            bias_out[:, hid] += jnp.sum(g_pre.astype(F32), axis=0, keepdims=True)
        branch = dot(act[pl.ds(at, step), :], w2[...], ((1,), (0,))) + bias2
        residual = band[pl.ds(2 * m, 2)].reshape(step, channels).astype(F32)
        result[pl.ds(2 * m, 2)] = (
            (residual + scale * branch).astype(BF16).reshape(2, cols, channels)
        )
        s_cot = s_cot + jnp.sum(upstream, axis=0, keepdims=True)
        s_scale = s_scale + jnp.sum(upstream * branch, axis=0, keepdims=True)
        g_norm = dot(pre[pl.ds(at, step), :], w1[...], ((1,), (1,)))
        standard = tmp[...]
        u = g_norm * gain
        g_conv = (
            u
            - jnp.mean(u, axis=-1, keepdims=True)
            - standard * jnp.mean(u * standard, axis=-1, keepdims=True)
        ) * inverse
        for h in range(halves):
            for k in range(2):
                dst = (h * rows + 2 * m + k) * pitch + LEAD
                grad[pl.ds(pl.multiple_of(dst, 8), cols), :] = g_conv[
                    k * cols : (k + 1) * cols, h * LANES : (h + 1) * LANES
                ]
        s_conv = s_conv + jnp.sum(g_conv, axis=0, keepdims=True)
        s_gain = s_gain + jnp.sum(g_norm * standard, axis=0, keepdims=True)
        s_norm = s_norm + jnp.sum(g_norm, axis=0, keepdims=True)
        return (s_conv, s_gain, s_norm, s_cot, s_scale)

    bias_out[...] = jnp.zeros_like(bias_out)
    zero = jnp.zeros((1, channels), F32)
    sums = lax.fori_loop(0, rows // 2, chunk, (zero,) * 5)
    sums = (sums[0], sums[1], sums[2], sums[3] * scale, sums[4])
    vecs[...] = jnp.concatenate(list(sums) + [zero] * 3, axis=0)

    keep_grad = pltpu.make_async_copy(grad, grad_out, sems.at[1])
    keep_grad.start()
    keep_result = pltpu.make_async_copy(result, result_out, sems.at[2])
    keep_result.start()

    even = (lax.axis_index("tile") & 1) == 0
    for n in range(tiles):
        hid = slice(n * 256, (n + 1) * 256)
        g_expand = dot(normed[...], pre[:, hid], ((0,), (0,)))
        g_reduce = dot(act[:, hid], gbr[...], ((0,), (0,)))
        mine[hid, :] = jnp.where(even, g_expand, g_reduce)
        other[hid, :] = jnp.where(even, g_reduce, g_expand).astype(BF16)

    def rim_half(h, carry):
        for k in range(6):
            acc = spread_row(grad, taps, h, k if k < 3 else rows + k, rows, pitch, groups)
            for j in range(groups):
                rim[pl.ds((h * 6 + k) * cpitch + j, SUB, stride=groups), :] = acc[j]
        return carry

    lax.fori_loop(0, halves, rim_half, 0)
    first = near == 0
    strip[...] = jnp.zeros_like(strip)
    for h in range(halves):
        lane = slice(h * LANES, (h + 1) * LANES)

        def column(c, h=h):
            return grad[pl.ds(h * rows * pitch + LEAD + c, SUB, stride=pitch), :]

        for side in range(2):
            edge = [column(c if side == 0 else cols - 1 - c) for c in range(3)]
            for d in range(3):
                slot = ((side * 3 + d) * halves + h) * 32
                for a in range(7):
                    total = none
                    for c in range(3 - d):
                        b = 2 - d - c if side == 0 else 4 + d + c
                        total = total + taps[h, a * 7 + b] * edge[c]
                    strip[slot + a : slot + a + SUB, :] += total
                for o in range(ext):
                    strip[slot + 16 + o : slot + 17 + o, :] = strip[
                        slot + ext - 1 - o : slot + ext - o, :
                    ]
        for d in range(3):
            slots = [((side * 3 + d) * halves + h) * 32 for side in range(2)]
            for turned in range(2):
                west, east = [strip[k + 16 * turned : k + 16 * turned + 16, :] for k in slots]
                one = jnp.where(first, west, east).astype(BF16)
                two = jnp.where(first, east, west).astype(BF16)
                if turned:
                    other[hidden + 16 * d : hidden + 16 * d + 16, lane] = one
                    other[hidden + 48 + 16 * d : hidden + 64 + 16 * d, lane] = two
                else:
                    plain_near[16 * d : 16 * d + 16, lane] = one
                    plain_far[16 * d : 16 * d + 16, lane] = two
    keep_pad.wait()
    keep_grad.wait()
    keep_result.wait()


def spread_row(grad, taps, h, o, rows, pitch, groups):
    acc = [jnp.zeros((SUB, LANES), F32)] * groups
    for a in range(7):
        if not 0 <= o - a < rows:
            continue
        src = (h * rows + o - a) * pitch + LEAD + 3
        tap = [taps[h, a * 7 + b] for b in range(7)]
        for jj in range(-6, groups):
            x = strided(grad, src + jj, groups)
            for b in range(7):
                if 0 <= jj + b < groups:
                    acc[jj + b] = acc[jj + b] + tap[b] * x
    return acc


def inner_kernel(h, grad, taps, out, token):
    token[...] = jnp.zeros_like(token)
    rows = 8
    cpitch = out.shape[0] // rows
    pitch = cpitch + LEAD
    groups = cpitch // SUB
    for r in range(rows):
        acc = spread_row(grad, taps, h, r + 3, rows, pitch, groups)
        for j in range(groups):
            out[pl.ds(r * cpitch + j, SUB, stride=groups), :] = acc[j]


def taps_kernel(h, grad, pad, out, token):
    token[...] = jnp.zeros_like(token)
    halves, rows = 2, 8
    ext = rows + 6
    pitch = (grad.shape[0] - SUB) // (halves * rows)
    wide = pad.shape[0] // (halves * ext)
    cols = pitch - 2 * LEAD
    groups = cols // SUB + 1

    def some(first, count):
        acc = [[jnp.zeros((SUB, LANES), F32)] * 7 for _ in range(count)]
        for i in range(rows + count - 1):
            base = (h * ext + i + first) * wide + LEAD - 3
            use = [k for k in range(count) if 0 <= i - k < rows]
            g = {}
            for jj in range(groups + 6):
                if jj < groups:
                    for k in use:
                        at = (h * rows + i - k) * pitch + LEAD + jj
                        g[k, jj] = strided(grad, at, groups)
                x = strided(pad, base + jj, groups)
                for b in range(7):
                    j = jj - b
                    if 0 <= j < groups:
                        for k in use:
                            acc[k][b] = acc[k][b] + g[k, j] * x
        for k in range(count):
            for b in range(7):
                out[pl.ds((first + k) * 7 + b, 1), :] = jnp.sum(acc[k][b], axis=0, keepdims=True)

    def pair(p, carry):
        some(2 * p, 2)
        return carry

    lax.fori_loop(0, 3, pair, 0)
    some(6, 1)


def rims_kernel(rim, got0, got1, got2, got3, match, within, across, token, total, held):
    token[...] = jnp.zeros_like(token)
    halves, _, cols, _ = within.shape
    even = (lax.axis_index("tile") & 1) == 0
    cpitch = rim.shape[0] // (halves * 6)
    near, turn_near, turn_far = gluing(match)
    arrived = unpack_columns(near, turn_near, turn_far, (got0, got1, got2, got3))
    for h in range(halves):
        for k in range(6):
            total[k * cols : (k + 1) * cols, :] = rim[
                (h * 6 + k) * cpitch : (h * 6 + k) * cpitch + cols, :
            ]
        for side in range(2):
            for d in range(3):
                held[...] = arrived(side, h, d)
                for k in range(6):
                    o = k if k < 3 else k + 8
                    at = k * cols + (d if side == 0 else cols - 1 - d)
                    total[at : at + 1, :] += held[o : o + 1, :]
        for k in range(3):
            top = total[k * cols : (k + 1) * cols, :].astype(BF16)
            bottom = total[(k + 3) * cols : (k + 4) * cols, :].astype(BF16)
            within[h, k] = jnp.where(even, bottom, top)
            across[h, k] = jnp.where(even, top, bottom)


def fields_kernel(inner0, inner1, within, across, got0, got1, got2, got3, cot, match, out, total, held):
    rows, cols, channels = cot.shape
    halves = channels // LANES
    cpitch = inner0.shape[0] // rows
    from_up, from_down = above_below(within, across)
    near, turn_near, turn_far = gluing(match)
    arrived = unpack_columns(near, turn_near, turn_far, (got0, got1, got2, got3))
    for h in range(halves):
        lane = slice(h * LANES, (h + 1) * LANES)
        for r in range(rows):
            at = r * cpitch
            own = (inner0, inner1)[h][at : at + cols, :] + cot[r, :, lane].astype(F32)
            if r < 3:
                own = own + from_up(h, r).astype(F32)
            if r >= rows - 3:
                own = own + from_down(h, r - rows + 3).astype(F32)
            total[r * cols : (r + 1) * cols, :] = own
        for side in range(2):
            for d in range(3):
                held[...] = arrived(side, h, d)
                at = pl.ds(d if side == 0 else cols - 1 - d, SUB, stride=cols)
                total[at, :] = total[at, :] + held[3 : 3 + rows, :]
        for r in range(rows):
            out[r, :, lane] = total[r * cols : (r + 1) * cols, :].astype(BF16)


def finish_kernel(factor, faces, chips, mine, peer, small, expand, reduce, g_taps, g_bias, vecs):
    hidden, channels = reduce.shape
    count = hidden // (faces * chips)
    face = lax.axis_index("face")
    chip = lax.axis_index("tile") >> 1
    even = (lax.axis_index("tile") & 1) == 0
    for f in range(faces):
        for z in range(chips):
            at = (f * chips + z) * count
            own = mine[at : at + count, :].astype(F32) * factor
            got = peer[at : at + count, :].astype(F32) * factor
            to = ((face ^ f) * chips + (chip ^ z)) * count
            reduce[pl.ds(pl.multiple_of(to, count), count), :] = jnp.where(even, got, own)
            row = pl.multiple_of(lax.rem(to, channels), count)
            col = pl.multiple_of((to // channels) * channels, channels)
            expand[pl.ds(row, count), pl.ds(col, channels)] = jnp.where(even, own, got)
    for a in range(7):
        g_taps[a] = small[a * 7 : a * 7 + 7, :] * factor
    for n in range(hidden // channels):
        g_bias[:, n * channels : (n + 1) * channels] = small[49 + n : 50 + n, :] * factor
    first = 49 + hidden // channels
    vecs[...] = small[first : first + 5, :] * factor


def face_swap(x, mask, turned=False):
    faces, tiles = lax.axis_size("face"), lax.axis_size("tile")
    pairs = [
        (f * tiles + t, (f ^ mask) * tiles + (tiles - 1 - t if turned else t))
        for f in range(faces)
        for t in range(tiles)
    ]
    return lax.ppermute(x, ("face", "tile"), pairs)


def glued_swap(strips):
    near_plain, near_turned, far_plain, far_turned = strips
    half = lax.axis_size("face") // 2
    return (
        face_swap(near_plain, 1),
        face_swap(near_turned, 1, True),
        face_swap(far_plain, half),
        face_swap(far_turned, half, True),
    )


def row_swap(within, across):
    count = lax.axis_size("tile")
    pairs = [(i, i + 1) for i in range(1, count - 1, 2)]
    return (
        swapped(within, "tile", 1),
        lax.ppermute(across, "tile", pairs + [(j, i) for i, j in pairs]),
    )


def above_below(within, across):
    even = (lax.axis_index("tile") & 1) == 0

    def up(*at):
        return jnp.where(even, across[at], within[at])

    def down(*at):
        return jnp.where(even, within[at], across[at])

    return up, down


def swapped(x, axis, mask):
    return lax.ppermute(x, axis, [(i, i ^ mask) for i in range(lax.axis_size(axis))])


def tree_sum(parts):
    parts = [p.astype(F32) for p in parts]
    while len(parts) > 1:
        parts = [parts[i] + parts[i + 1] for i in range(0, len(parts), 2)]
    return parts[0]


def joined(x, riders):
    return jnp.concatenate([x] + list(riders), 0) if riders else x


def scatter_start(x, axis, masks, index, riders):
    shares = x.reshape((len(masks) + 1, x.shape[0] // (len(masks) + 1)) + x.shape[1:])
    step = masks[0]
    cut = shares.shape[1]
    own = lax.dynamic_index_in_dim(shares, index, 0, keepdims=False)
    sent = [
        lax.dynamic_index_in_dim(shares, index ^ (m // step), 0, keepdims=False).astype(BF16)
        for m in masks
    ]
    got = [swapped(joined(v, riders.get(m)), axis, m) for v, m in zip(sent, masks)]
    return [own] + [g[:cut] for g in got], {m: got[masks.index(m)][cut:] for m in riders}


def gather_start(x, small, axis, masks):
    sent = jnp.concatenate([x, small.astype(BF16)], 0)
    return [swapped(sent, axis, m) for m in masks]


def gather_done(x, small, got):
    cut = x.shape[0]
    pieces = jnp.concatenate([x] + [g[:cut] for g in got], 0)
    return pieces, tree_sum([small.astype(BF16)] + [g[cut:] for g in got])


def ordered(x, token):
    blocks = x.reshape(x.shape[0] // SUB, SUB, x.shape[1] // LANES, LANES)
    return (blocks + token[None, :, None, :]).reshape(x.shape)


def shards(
    fields,
    cotangent,
    edge_match,
    depth_kernel,
    depth_bias,
    norm_gain,
    norm_bias,
    expand_weight,
    expand_bias,
    reduce_weight,
    reduce_bias,
    layer_scale,
):
    band = fields[0]
    cot = cotangent[0]
    rows, cols, channels = band.shape
    halves = channels // LANES
    hidden = expand_weight.shape[1]
    pitch = cols + 2 * LEAD
    wide = pitch + SUB
    ext = rows + 6
    cells = rows * cols
    faces, tiles = lax.axis_size("face"), lax.axis_size("tile")
    shape = jax.ShapeDtypeStruct
    strips = [shape((48, channels), BF16)] * 4

    *rim_rows, columns = call(
        ends_kernel,
        [
            shape((3, cols, channels), BF16),
            shape((3, cols, channels), BF16),
            shape((rows, 32, channels), BF16),
        ],
        [],
        1_000_000_000,
        (band,),
    )
    beside = row_swap(*rim_rows)
    sides = call(
        edges_kernel,
        strips,
        [pltpu.VMEM((2, 16 * SUB, LANES), F32)],
        900_000_000,
        (columns, *beside, edge_match),
        smem=1,
    )
    got = glued_swap(sides)
    part, taps = call(
        own_rows_kernel,
        [
            pltpu.VMEM((halves * rows * (cols + SUB), LANES), F32),
            pltpu.VMEM((halves, 50, SUB, LANES), F32),
        ],
        [pltpu.VMEM((halves * ext * wide, LANES), F32)],
        4_500_000_000,
        (band, depth_kernel, depth_bias[None]),
        limit=4,
        after=(sides[0],),
    )
    part, taps = kept(part), kept(taps)
    sign = shape((SUB, LANES), F32)
    result, pad, grad, mine, other, plain_near, plain_far, rim, vecs, bias_out = call(
        forward_kernel,
        [
            pltpu.HBM(band.shape, BF16),
            pltpu.HBM((halves * ext * wide, LANES), F32),
            pltpu.HBM((halves * rows * pitch + SUB, LANES), F32),
            shape((hidden, channels), F32),
            shape((hidden + 96, channels), BF16),
            shape((48, channels), BF16),
            shape((48, channels), BF16),
            shape((halves * 6 * (cols + SUB), LANES), F32),
            shape((8, channels), F32),
            shape((1, hidden), F32),
        ],
        [
            pltpu.VMEM(band.shape, BF16),
            pltpu.VMEM((halves * ext * wide, LANES), F32),
            pltpu.VMEM((halves * rows * pitch + SUB, LANES), F32),
            pltpu.VMEM((halves * rows * (cols + SUB), LANES), F32),
            pltpu.VMEM((cells, channels), BF16),
            pltpu.VMEM((cells, hidden), BF16),
            pltpu.VMEM((cells, hidden), BF16),
            pltpu.VMEM((cells, channels), BF16),
            pltpu.VMEM((2 * cols, channels), F32),
            pltpu.VMEM((12 * 32, LANES), F32),
            pltpu.SemaphoreType.DMA((3,)),
        ],
        12_000_000_000,
        (
            band, *beside, *got, cot, taps, norm_gain[None], norm_bias[None], reduce_bias[None],
            layer_scale[None], expand_bias.reshape(1, hidden), expand_weight, reduce_weight, part,
            edge_match,
        ),
        smem=1,
        limit=20,
        left=(0, 1, 2),
    )

    face_masks = list(range(1, faces))
    chip_masks = list(range(2, tiles, 2))
    half, mirror = faces // 2, tiles - 2
    peer = swapped(other, "tile", 1)
    turned_near, turned_far = peer[hidden : hidden + 48], peer[hidden + 48 :]

    def half_taps(h, after):
        return call(
            lambda *refs: taps_kernel(h, *refs),
            [shape((56, LANES), F32), sign],
            [],
            3_500_000_000,
            (grad, pad),
            after=after,
        )

    riders = {1: [plain_near, turned_near], half: [plain_far, turned_far]}
    total = (mine + peer[:hidden].astype(F32)).astype(BF16)
    got, rode = scatter_start(total, "face", face_masks, lax.axis_index("face"), riders)
    taps0, token = half_taps(0, (turned_near,))
    share = ordered(tree_sum(got), token)
    plain_near, turned_near = rode[1][:48], rode[1][48:]
    plain_far, turned_far = rode[half][:48], rode[half][48:]
    riders = {mirror: [turned_near, turned_far]}
    got, rode = scatter_start(share, "tile", chip_masks, lax.axis_index("tile") >> 1, riders)
    taps1, token = half_taps(1, (got[1],))
    share = ordered(tree_sum(got), token).astype(BF16)
    columns = (plain_near, rode[mirror][:48], plain_far, rode[mirror][48:])
    small = jnp.concatenate(
        [
            jnp.concatenate([taps0[:49], taps1[:49]], 1),
            bias_out.reshape(hidden // channels, channels),
            vecs[0:5],
            jnp.zeros((SMALL - 54 - hidden // channels, channels), F32),
        ],
        0,
    )
    def half_inner(h, after):
        return call(
            lambda *refs: inner_kernel(h, *refs),
            [shape((rows * (cols + SUB), LANES), F32), sign],
            [],
            2_100_000_000,
            (grad, taps),
            after=after,
        )

    got = gather_start(share, small, "tile", chip_masks)
    within, across, token = call(
        rims_kernel,
        [shape((halves, 3, cols, LANES), BF16)] * 2 + [sign],
        [pltpu.VMEM((6 * cols, LANES), F32), pltpu.VMEM((16, LANES), F32)],
        900_000_000,
        (rim, *columns, edge_match),
        smem=1,
    )
    inner0, token = half_inner(0, (token, got[0]))
    arrived = row_swap(within, across)
    pieces, small = gather_done(share, small, got)
    small = ordered(small, token)
    got = gather_start(pieces, small, "face", face_masks)
    inner1, token = half_inner(1, (got[0], arrived[1]))
    pieces, small = gather_done(pieces, small, got)
    small = ordered(small, token).astype(BF16)
    peer = swapped(jnp.concatenate([pieces, small], 0), "tile", 1)
    (grad_fields,) = call(
        fields_kernel,
        [shape(band.shape, BF16)],
        [pltpu.VMEM((cells, LANES), F32), pltpu.VMEM((16, LANES), F32)],
        2_000_000_000,
        (inner0, inner1, *arrived, *columns, cot, edge_match),
        smem=1,
    )
    small = small.astype(F32) + peer[hidden:].astype(F32)

    factor = 1.0 / math.sqrt(faces * tiles * cells)

    def finish(*refs):
        finish_kernel(factor, faces, tiles // 2, *refs)

    g_expand, g_reduce, g_taps, g_bias, g_vecs = call(
        finish,
        [
            shape((channels, hidden), F32),
            shape((hidden, channels), F32),
            shape((7, 7, channels), F32),
            shape((1, hidden), F32),
            shape((5, channels), F32),
        ],
        [],
        2_000_000_000,
        (pieces, peer[:hidden], small),
    )
    return (
        result[None],
        grad_fields[None],
        g_taps,
        g_expand,
        g_reduce,
        g_bias.reshape(hidden),
        g_vecs,
    )


def solution(mesh):
    return jax.shard_map(
        shards,
        mesh=mesh,
        in_specs=(P("face", "tile"), P("face", "tile")) + (P(),) * 10,
        out_specs=(P("face", "tile"), P("face", "tile")) + (P(),) * 5,
        check_vma=False,
    )
```

```python
import math

import jax
import jax.numpy as jnp
from jax import lax
from jax.experimental import pallas as pl
from jax.experimental.pallas import tpu as pltpu
from jax.sharding import PartitionSpec as P

EPSILON = 1e-06
ROOT_COEF = 0.7978845608028654
CUBIC_COEF = 0.044715
LANES = 128
SUB = 8
LEAD = 8
SMALL = 64
F32 = jnp.float32
BF16 = jnp.bfloat16


def dot(a, b, dims):
    return lax.dot_general(a, b, (dims, ((), ())), preferred_element_type=F32)


def call(body, outs, scratch, flops, args, smem=0, after=(), limit=4, left=()):
    vmem = pl.BlockSpec(memory_space=pltpu.VMEM)
    scalar = pl.BlockSpec(memory_space=pltpu.SMEM)
    anywhere = pl.BlockSpec(memory_space=pl.ANY)
    outside = pl.BlockSpec(memory_space=pltpu.HBM)
    count = len(args)

    def run(*refs):
        body(*refs[:count], *refs[count + len(after) :])

    return pl.pallas_call(
        run,
        out_shape=outs,
        in_specs=[vmem] * (count - smem) + [scalar] * smem + [anywhere] * len(after),
        out_specs=[outside if i in left else vmem for i in range(len(outs))],
        scratch_shapes=scratch,
        compiler_params=pltpu.CompilerParams(vmem_limit_bytes=limit * 1024 * 1024),
        cost_estimate=pl.CostEstimate(flops=flops, bytes_accessed=1 << 20, transcendentals=0),
    )(*args, *after)


def kept(x):
    return pltpu.with_memory_space_constraint(x, pltpu.VMEM)


def strided(ref, start, groups):
    return ref[pl.ds(start, SUB, stride=groups), :]


def gluing(match, flags):
    face = lax.axis_index("face")
    near = jnp.where(match[face, 0, 0] == face ^ 1, 0, 1)
    flags[...] = jnp.zeros_like(flags)
    for k, value in enumerate((near, match[face, near, 2], match[face, 1 - near, 2])):
        flags[k : k + 1, :] = jnp.full((1, LANES), value, jnp.int32).astype(F32)


def glued(flags):
    return flags[0:1, :] == 0.0, flags[1:2, :] == 1.0, flags[2:3, :] == 1.0


def pack_columns(tile, count, first, held, outs):
    vals = {}
    for side in range(2):
        for h in range(2):
            held[...] = jnp.zeros_like(held)
            for i in range(count):
                t = tile(side, h, i)
                held[0, i * SUB : (i + 1) * SUB, :] = t
                held[1, (count - 1 - i) * SUB : (count - i) * SUB, :] = t
            for v in range(2):
                for d in range(3):
                    vals[side, h, v, d] = held[v, pl.ds(tile.column(side, d), 16, stride=SUB), :]
    for h in range(2):
        lane = slice(h * LANES, (h + 1) * LANES)
        for v in range(2):
            for d in range(3):
                west, east = vals[0, h, v, d], vals[1, h, v, d]
                at = slice(d * 16, d * 16 + 16)
                outs[v][at, lane] = jnp.where(first, west, east).astype(BF16)
                outs[2 + v][at, lane] = jnp.where(first, east, west).astype(BF16)


def unpack_columns(first, turn_near, turn_far, got):
    def value(side, h, d):
        lane = slice(h * LANES, (h + 1) * LANES)
        parts = [g[d * 16 : d * 16 + 16, lane].astype(F32) for g in got]
        one = jnp.where(turn_near, parts[1], parts[0])
        two = jnp.where(turn_far, parts[3], parts[2])
        return jnp.where(first, one, two) if side == 0 else jnp.where(first, two, one)

    return value


def ends_kernel(band, within, across, columns):
    rows, cols, _ = band.shape
    even = (lax.axis_index("tile") & 1) == 0
    for k in range(3):
        top, bottom = band[k], band[rows - 3 + k]
        within[k] = jnp.where(even, bottom, top)
        across[k] = jnp.where(even, top, bottom)
    for r in range(rows):
        columns[r, 0:16, :] = band[r, 0:16, :]
        columns[r, 16:32, :] = band[r, cols - 16 : cols, :]


def edges_kernel(columns, within, across, match, *refs):
    outs, flags, held = refs[:4], refs[4], refs[5]
    gluing(match, flags)
    up, down = above_below(within, across)
    rows, _, _ = columns.shape
    _, cols, _ = within.shape
    first, _, _ = glued(flags)

    def tile(side, h, i):
        lane = slice(h * LANES, (h + 1) * LANES)
        at = slice(0, 16) if side == 0 else slice(cols - 16, cols)
        if i < 3:
            v = up(i, at, lane)
        elif i < rows + 3:
            v = columns[i - 3, slice(0, 16) if side == 0 else slice(16, 32), lane]
        else:
            v = down(i - rows - 3, at, lane)
        return v.astype(F32)[0:SUB] if side == 0 else v.astype(F32)[SUB:16]

    tile.column = lambda side, d: d if side == 0 else SUB - 1 - d
    pack_columns(tile, rows + 6, first, held, outs)


def fill_pad(pad, halves, ext, wide, cols, source, which):
    for h in range(halves):
        lane = slice(h * LANES, (h + 1) * LANES)
        for i in which:
            at = (h * ext + i) * wide
            pad[at : at + LEAD, :] = jnp.zeros((LEAD, LANES), F32)
            pad[at + LEAD : at + LEAD + cols, :] = source(i, lane).astype(F32)
            pad[at + LEAD + cols : at + wide, :] = jnp.zeros((LEAD + SUB, LANES), F32)


def own_rows_kernel(band, kernel, bias, conv, taps, pad):
    for h in range(2):
        lane = slice(h * LANES, (h + 1) * LANES)
        for a in range(7):
            row = kernel[a].astype(F32)
            for b in range(7):
                taps[h, a * 7 + b] = jnp.broadcast_to(row[b : b + 1, lane], (SUB, LANES))
        taps[h, 49] = jnp.broadcast_to(bias[:, lane], (SUB, LANES))
    rows, cols, channels = band.shape
    halves = channels // LANES
    pitch = cols + 2 * LEAD
    wide = pitch + SUB
    ext = rows + 6
    groups = cols // SUB + 1
    cpitch = groups * SUB
    fill_pad(pad, halves, ext, wide, cols, lambda i, lane: band[i - 3, :, lane], range(3, rows + 3))

    def half(h, carry):
        for r in range(rows):
            acc = [taps[h, 49]] * groups
            for a in range(7):
                if not 3 <= r + a < rows + 3:
                    continue
                base = (h * ext + r + a) * wide + LEAD - 3
                tap = [taps[h, a * 7 + b] for b in range(7)]
                for jj in range(groups + 6):
                    x = strided(pad, base + jj, groups)
                    for b in range(7):
                        if 0 <= jj - b < groups:
                            acc[jj - b] = acc[jj - b] + tap[b] * x
            for j in range(groups):
                conv[pl.ds((h * rows + r) * cpitch + j, SUB, stride=groups), :] = acc[j]
        return carry

    lax.fori_loop(0, halves, half, 0)


def forward_kernel(
    band, within, across, got0, got1, got2, got3, cot, taps, gain, shift, bias2, scale, bias1, w1, w2, part, flags,
    result_out, pad_out, grad_out, mine, other, plain_near, plain_far, rim_out, vecs, bias_out,
    rim, result, pad, grad, conv, normed, act, pre, gbr, tmp, strip, sems,
):
    rows, cols, channels = band.shape
    halves = channels // LANES
    pitch = cols + 2 * LEAD
    wide = pitch + SUB
    ext = rows + 6
    groups = cols // SUB + 1
    cpitch = groups * SUB
    hidden = w1.shape[1]

    first, turn_near, turn_far = glued(flags)
    arrived = unpack_columns(first, turn_near, turn_far, (got0, got1, got2, got3))

    up, down = above_below(within, across)

    def source(i, lane):
        if i < 3:
            return up(i, slice(None), lane)
        return band[i - 3, :, lane] if i < rows + 3 else down(i - rows - 3, slice(None), lane)

    fill_pad(pad, halves, ext, wide, cols, source, range(ext))
    for h in range(halves):
        for d in range(3):
            for side in range(2):
                col = LEAD - 1 - d if side == 0 else LEAD + cols + d
                v = arrived(side, h, d)
                at = h * ext * wide + col
                pad[pl.ds(at, SUB, stride=wide), :] = v[0:SUB]
                pad[pl.ds(at + SUB * wide, ext - SUB, stride=wide), :] = v[SUB:ext]
        for r in range(rows):
            at = (h * rows + r) * pitch
            grad[at : at + LEAD, :] = jnp.zeros((LEAD, LANES), F32)
            grad[at + LEAD + cols : at + pitch, :] = jnp.zeros((LEAD, LANES), F32)

    keep_pad = pltpu.make_async_copy(pad, pad_out, sems.at[0])
    keep_pad.start()
    tail = halves * rows * pitch
    grad[tail : tail + SUB, :] = jnp.zeros((SUB, LANES), F32)

    where = lax.broadcasted_iota(jnp.int32, (SUB, LANES), 0)
    at_west, at_east = where == 0, where == SUB - 1
    none = jnp.zeros((SUB, LANES), F32)
    over = cols + 3 - (SUB - 1) * groups

    def complete(h, carry):
        for r in range(rows):
            acc = [strided(part, (h * rows + r) * cpitch + j, groups) for j in range(groups)]
            for a in range(7):
                base = (h * ext + r + a) * wide + LEAD - 3
                tap = [taps[h, a * 7 + b] for b in range(7)]
                if not 3 <= r + a < rows + 3:
                    for jj in range(groups + 6):
                        x = strided(pad, base + jj, groups)
                        for b in range(7):
                            if 0 <= jj - b < groups:
                                acc[jj - b] = acc[jj - b] + tap[b] * x
                    continue
                for d in range(3):
                    x = jnp.where(at_west, strided(pad, base + d, groups), none)
                    for b in range(d + 1):
                        acc[d - b] = acc[d - b] + tap[b] * x
                    x = jnp.where(at_east, strided(pad, base + over + d, groups), none)
                    for b in range(4 + d, 7):
                        acc[over + d - b] = acc[over + d - b] + tap[b] * x
            for j in range(groups):
                conv[pl.ds((h * rows + r) * cpitch + j, SUB, stride=groups), :] = acc[j]
        return carry

    lax.fori_loop(0, halves, complete, 0)

    step = 2 * cols
    gain, shift, bias2, scale = gain[...], shift[...], bias2[...], scale[...]
    tiles = hidden // 256

    def chunk(m, carry):
        s_conv, s_gain, s_norm, s_cot, s_scale = carry
        at = pl.multiple_of(m * step, step)
        x = jnp.concatenate(
            [
                jnp.concatenate(
                    [
                        conv[pl.ds(pl.multiple_of((h * rows + 2 * m + k) * cpitch, 8), cols), :]
                        for k in range(2)
                    ],
                    axis=0,
                )
                for h in range(halves)
            ],
            axis=1,
        )
        centred = x - jnp.mean(x, axis=-1, keepdims=True)
        inverse = lax.rsqrt(jnp.mean(centred * centred, axis=-1, keepdims=True) + EPSILON)
        standard = centred * inverse
        lane_in = (standard * gain + shift).astype(BF16)
        normed[pl.ds(at, step), :] = lane_in
        tmp[...] = standard
        upstream = cot[pl.ds(2 * m, 2)].reshape(step, channels).astype(F32)
        g_branch = (upstream * scale).astype(BF16)
        gbr[pl.ds(at, step), :] = g_branch
        for n in range(tiles):
            hid = slice(n * 256, (n + 1) * 256)
            v = dot(lane_in, w1[:, hid], ((1,), (0,))) + bias1[:, hid]
            v2 = v * v
            half = 0.5 + 0.5 * jnp.tanh(v * (ROOT_COEF + ROOT_COEF * CUBIC_COEF * v2))
            act[pl.ds(at, step), hid] = (v * half).astype(BF16)
            slope = half * (
                1.0 + (1.0 - half) * (v * (2 * ROOT_COEF + 6 * ROOT_COEF * CUBIC_COEF * v2))
            )
            d_act = dot(g_branch, w2[hid, :], ((1,), (1,)))
            g_pre = (d_act * slope).astype(BF16)
            pre[pl.ds(at, step), hid] = g_pre
            bias_out[:, hid] += jnp.sum(g_pre.astype(F32), axis=0, keepdims=True)
        branch = dot(act[pl.ds(at, step), :], w2[...], ((1,), (0,))) + bias2
        residual = band[pl.ds(2 * m, 2)].reshape(step, channels).astype(F32)
        result[pl.ds(2 * m, 2)] = (
            (residual + scale * branch).astype(BF16).reshape(2, cols, channels)
        )
        s_cot = s_cot + jnp.sum(upstream, axis=0, keepdims=True)
        s_scale = s_scale + jnp.sum(upstream * branch, axis=0, keepdims=True)
        g_norm = dot(pre[pl.ds(at, step), :], w1[...], ((1,), (1,)))
        standard = tmp[...]
        u = g_norm * gain
        g_conv = (
            u
            - jnp.mean(u, axis=-1, keepdims=True)
            - standard * jnp.mean(u * standard, axis=-1, keepdims=True)
        ) * inverse
        for h in range(halves):
            for k in range(2):
                dst = (h * rows + 2 * m + k) * pitch + LEAD
                grad[pl.ds(pl.multiple_of(dst, 8), cols), :] = g_conv[
                    k * cols : (k + 1) * cols, h * LANES : (h + 1) * LANES
                ]
        s_conv = s_conv + jnp.sum(g_conv, axis=0, keepdims=True)
        s_gain = s_gain + jnp.sum(g_norm * standard, axis=0, keepdims=True)
        s_norm = s_norm + jnp.sum(g_norm, axis=0, keepdims=True)
        return (s_conv, s_gain, s_norm, s_cot, s_scale)

    bias_out[...] = jnp.zeros_like(bias_out)
    zero = jnp.zeros((1, channels), F32)
    sums = lax.fori_loop(0, rows // 2, chunk, (zero,) * 5)
    sums = (sums[0], sums[1], sums[2], sums[3] * scale, sums[4])
    vecs[...] = jnp.concatenate(list(sums) + [zero] * 3, axis=0)

    keep_grad = pltpu.make_async_copy(grad, grad_out, sems.at[1])
    keep_grad.start()
    keep_result = pltpu.make_async_copy(result, result_out, sems.at[2])
    keep_result.start()

    def rim_half(h, carry):
        for k in range(6):
            acc = spread_row(grad, taps, h, k if k < 3 else rows + k, rows, pitch, groups)
            for j in range(groups):
                rim[pl.ds((h * 6 + k) * cpitch + j, SUB, stride=groups), :] = acc[j]
        return carry

    lax.fori_loop(0, halves, rim_half, 0)
    keep_rim = pltpu.make_async_copy(rim, rim_out, sems.at[3])
    keep_rim.start()
    strip[...] = jnp.zeros_like(strip)
    for h in range(halves):
        lane = slice(h * LANES, (h + 1) * LANES)

        def column(c, h=h):
            return grad[pl.ds(h * rows * pitch + LEAD + c, SUB, stride=pitch), :]

        for side in range(2):
            edge = [column(c if side == 0 else cols - 1 - c) for c in range(3)]
            for d in range(3):
                slot = ((side * 3 + d) * halves + h) * 32
                for a in range(7):
                    total = none
                    for c in range(3 - d):
                        b = 2 - d - c if side == 0 else 4 + d + c
                        total = total + taps[h, a * 7 + b] * edge[c]
                    strip[slot + a : slot + a + SUB, :] += total
                for o in range(ext):
                    strip[slot + 16 + o : slot + 17 + o, :] = strip[
                        slot + ext - 1 - o : slot + ext - o, :
                    ]
        for d in range(3):
            slots = [((side * 3 + d) * halves + h) * 32 for side in range(2)]
            for turned in range(2):
                west, east = [strip[k + 16 * turned : k + 16 * turned + 16, :] for k in slots]
                one = jnp.where(first, west, east).astype(BF16)
                two = jnp.where(first, east, west).astype(BF16)
                if turned:
                    other[hidden + 16 * d : hidden + 16 * d + 16, lane] = one
                    other[hidden + 48 + 16 * d : hidden + 64 + 16 * d, lane] = two
                else:
                    plain_near[16 * d : 16 * d + 16, lane] = one
                    plain_far[16 * d : 16 * d + 16, lane] = two

    even = (lax.axis_index("tile") & 1) == 0
    for n in range(tiles):
        hid = slice(n * 256, (n + 1) * 256)
        g_expand = dot(normed[...], pre[:, hid], ((0,), (0,)))
        g_reduce = dot(act[:, hid], gbr[...], ((0,), (0,)))
        mine[hid, :] = jnp.where(even, g_expand, g_reduce)
        other[hid, :] = jnp.where(even, g_reduce, g_expand).astype(BF16)
    keep_pad.wait()
    keep_grad.wait()
    keep_result.wait()
    keep_rim.wait()


def spread_row(grad, taps, h, o, rows, pitch, groups):
    acc = [jnp.zeros((SUB, LANES), F32)] * groups
    for a in range(7):
        if not 0 <= o - a < rows:
            continue
        src = (h * rows + o - a) * pitch + LEAD + 3
        tap = [taps[h, a * 7 + b] for b in range(7)]
        for jj in range(-6, groups):
            x = strided(grad, src + jj, groups)
            for b in range(7):
                if 0 <= jj + b < groups:
                    acc[jj + b] = acc[jj + b] + tap[b] * x
    return acc


def inner_kernel(h, grad, taps, out, token):
    token[...] = jnp.zeros_like(token)
    rows = 8
    cpitch = out.shape[0] // rows
    pitch = cpitch + LEAD
    groups = cpitch // SUB
    for r in range(rows):
        acc = spread_row(grad, taps, h, r + 3, rows, pitch, groups)
        for j in range(groups):
            out[pl.ds(r * cpitch + j, SUB, stride=groups), :] = acc[j]


def taps_kernel(h, grad, pad, out, token):
    token[...] = jnp.zeros_like(token)
    halves, rows = 2, 8
    ext = rows + 6
    pitch = (grad.shape[0] - SUB) // (halves * rows)
    wide = pad.shape[0] // (halves * ext)
    cols = pitch - 2 * LEAD
    groups = cols // SUB + 1

    def some(first, count):
        acc = [[jnp.zeros((SUB, LANES), F32)] * 7 for _ in range(count)]
        for i in range(rows + count - 1):
            base = (h * ext + i + first) * wide + LEAD - 3
            use = [k for k in range(count) if 0 <= i - k < rows]
            g = {}
            for jj in range(groups + 6):
                if jj < groups:
                    for k in use:
                        at = (h * rows + i - k) * pitch + LEAD + jj
                        g[k, jj] = strided(grad, at, groups)
                x = strided(pad, base + jj, groups)
                for b in range(7):
                    j = jj - b
                    if 0 <= j < groups:
                        for k in use:
                            acc[k][b] = acc[k][b] + g[k, j] * x
        for k in range(count):
            for b in range(7):
                out[pl.ds((first + k) * 7 + b, 1), :] = jnp.sum(acc[k][b], axis=0, keepdims=True)

    def pair(p, carry):
        some(2 * p, 2)
        return carry

    lax.fori_loop(0, 3, pair, 0)
    some(6, 1)


def rims_kernel(rim, got0, got1, got2, got3, flags, within, across, token, total, held):
    token[...] = jnp.zeros_like(token)
    halves, _, cols, _ = within.shape
    even = (lax.axis_index("tile") & 1) == 0
    cpitch = rim.shape[0] // (halves * 6)
    first, turn_near, turn_far = glued(flags)
    arrived = unpack_columns(first, turn_near, turn_far, (got0, got1, got2, got3))
    for h in range(halves):
        for k in range(6):
            total[k * cols : (k + 1) * cols, :] = rim[
                (h * 6 + k) * cpitch : (h * 6 + k) * cpitch + cols, :
            ]
        for side in range(2):
            for d in range(3):
                held[...] = arrived(side, h, d)
                for k in range(6):
                    o = k if k < 3 else k + 8
                    at = k * cols + (d if side == 0 else cols - 1 - d)
                    total[at : at + 1, :] += held[o : o + 1, :]
        for k in range(3):
            top = total[k * cols : (k + 1) * cols, :].astype(BF16)
            bottom = total[(k + 3) * cols : (k + 4) * cols, :].astype(BF16)
            within[h, k] = jnp.where(even, bottom, top)
            across[h, k] = jnp.where(even, top, bottom)


def fields_kernel(inner0, inner1, within, across, got0, got1, got2, got3, cot, flags, out, token, total, held):
    token[...] = jnp.zeros_like(token)
    rows, cols, channels = cot.shape
    halves = channels // LANES
    cpitch = inner0.shape[0] // rows
    from_up, from_down = above_below(within, across)
    first, turn_near, turn_far = glued(flags)
    arrived = unpack_columns(first, turn_near, turn_far, (got0, got1, got2, got3))
    for h in range(halves):
        lane = slice(h * LANES, (h + 1) * LANES)
        for r in range(rows):
            at = r * cpitch
            own = (inner0, inner1)[h][at : at + cols, :] + cot[r, :, lane].astype(F32)
            if r < 3:
                own = own + from_up(h, r).astype(F32)
            if r >= rows - 3:
                own = own + from_down(h, r - rows + 3).astype(F32)
            total[r * cols : (r + 1) * cols, :] = own
        for side in range(2):
            for d in range(3):
                held[...] = arrived(side, h, d)
                at = pl.ds(d if side == 0 else cols - 1 - d, SUB, stride=cols)
                total[at, :] = total[at, :] + held[3 : 3 + rows, :]
        for r in range(rows):
            out[r, :, lane] = total[r * cols : (r + 1) * cols, :].astype(BF16)


def merge_kernel(masks, half, mine, peer, plain_near, plain_far, flags, own, token, *messages):
    _, turn_near, turn_far = glued(flags)
    token[...] = jnp.zeros_like(token)
    hidden = mine.shape[0]
    count = own.shape[0]
    face = lax.axis_index("face")

    def share(mask):
        at = pl.ds(pl.multiple_of((face ^ mask) * count, count), count)
        return mine[at, :] + peer[at, :].astype(F32)

    def choose(turn, at, plain, message):
        for h in range(2):
            lane = slice(h * LANES, (h + 1) * LANES)
            turned = peer[at : at + 48, lane].astype(F32)
            message[count : count + 48, lane] = jnp.where(
                turn, turned, plain[:, lane].astype(F32)
            ).astype(BF16)

    own[...] = share(0)
    for mask, message in zip(masks, messages):
        message[0:count, :] = share(mask).astype(BF16)
        if mask == 1:
            choose(turn_near, hidden, plain_near, message)
        if mask == half:
            choose(turn_far, hidden + 48, plain_far, message)


def deal_kernel(masks, mirror, near, far, own, *refs):
    count = own.shape[0]
    got, (part, token, *messages), total = refs[: len(refs) - 3 - len(masks)], refs[
        len(refs) - 3 - len(masks) : -1
    ], refs[-1]
    token[...] = jnp.zeros_like(token)
    size = part.shape[0]
    chip = lax.axis_index("tile") >> 1
    total[...] = tree_sum([own[...]] + [g[0:count, :] for g in got])

    def share(place):
        return total[pl.ds(pl.multiple_of(place * size, size), size), :]

    part[...] = share(chip)
    for mask, message in zip(masks, messages):
        at = 0
        if mask == mirror:
            message[0:48, :] = got[near][count:, :]
            message[48:96, :] = got[far][count:, :]
            at = 96
        message[at : at + size, :] = share(chip ^ (mask >> 1)).astype(BF16)


def pack_shares_kernel(own, *refs):
    *got, taps0, taps1, bias, vecs, out, held = refs
    count, channels = own.shape
    held[...] = jnp.zeros_like(held)
    held[0:49, 0:LANES] = taps0[0:49, :]
    held[0:49, LANES : 2 * LANES] = taps1[0:49, :]
    parts = bias.shape[1] // channels
    for n in range(parts):
        held[49 + n : 50 + n, :] = bias[:, n * channels : (n + 1) * channels]
    held[49 + parts : 54 + parts, :] = vecs[0:5, :]
    out[0:SMALL, :] = held[...].astype(BF16)
    out[SMALL:, :] = tree_sum([own[...]] + [g[0:count, :] for g in got]).astype(BF16)


def pack_pieces_kernel(own, *refs):
    *got, out = refs
    parts = [own[...].astype(F32)] + [g[...].astype(F32) for g in got]
    out[0:SMALL, :] = tree_sum([p[0:SMALL] for p in parts]).astype(BF16)
    out[SMALL:, :] = jnp.concatenate([p[SMALL:] for p in parts], 0).astype(BF16)


def finish_kernel(factor, faces, chips, mine, peer, expand, reduce, g_taps, g_bias, vecs):
    hidden, channels = reduce.shape
    count = hidden // (faces * chips)
    face = lax.axis_index("face")
    chip = lax.axis_index("tile") >> 1
    even = (lax.axis_index("tile") & 1) == 0
    small = mine[0:SMALL, :].astype(F32) + peer[0:SMALL, :].astype(F32)
    small = small * factor
    for f in range(faces):
        for z in range(chips):
            at = SMALL + (f * chips + z) * count
            own = mine[at : at + count, :].astype(F32) * factor
            got = peer[at : at + count, :].astype(F32) * factor
            to = ((face ^ f) * chips + (chip ^ z)) * count
            reduce[pl.ds(pl.multiple_of(to, count), count), :] = jnp.where(even, got, own)
            row = pl.multiple_of(lax.rem(to, channels), count)
            col = pl.multiple_of((to // channels) * channels, channels)
            expand[pl.ds(row, count), pl.ds(col, channels)] = jnp.where(even, own, got)
    for a in range(7):
        g_taps[a] = small[a * 7 : a * 7 + 7, :]
    for n in range(hidden // channels):
        g_bias[:, n * channels : (n + 1) * channels] = small[49 + n : 50 + n, :]
    first = 49 + hidden // channels
    vecs[...] = small[first : first + 5, :]


def face_swap(x, mask, turned=False):
    faces, tiles = lax.axis_size("face"), lax.axis_size("tile")
    pairs = [
        (f * tiles + t, (f ^ mask) * tiles + (tiles - 1 - t if turned else t))
        for f in range(faces)
        for t in range(tiles)
    ]
    return lax.ppermute(x, ("face", "tile"), pairs)


def glued_swap(strips):
    near_plain, near_turned, far_plain, far_turned = strips
    half = lax.axis_size("face") // 2
    return (
        face_swap(near_plain, 1),
        face_swap(near_turned, 1, True),
        face_swap(far_plain, half),
        face_swap(far_turned, half, True),
    )


def row_swap(within, across):
    count = lax.axis_size("tile")
    pairs = [(i, i + 1) for i in range(1, count - 1, 2)]
    return (
        swapped(within, "tile", 1),
        lax.ppermute(across, "tile", pairs + [(j, i) for i, j in pairs]),
    )


def above_below(within, across):
    even = (lax.axis_index("tile") & 1) == 0

    def up(*at):
        return jnp.where(even, across[at], within[at])

    def down(*at):
        return jnp.where(even, within[at], across[at])

    return up, down


def swapped(x, axis, mask):
    return lax.ppermute(x, axis, [(i, i ^ mask) for i in range(lax.axis_size(axis))])


def tree_sum(parts):
    parts = [p.astype(F32) for p in parts]
    while len(parts) > 1:
        parts = [parts[i] + parts[i + 1] for i in range(0, len(parts), 2)]
    return parts[0]


def gathered(x, axis, masks):
    got = [swapped(x, axis, m) for m in masks]
    return [x] + [got[masks.index(m)] for m in sorted(masks)]


def shards(
    fields,
    cotangent,
    edge_match,
    depth_kernel,
    depth_bias,
    norm_gain,
    norm_bias,
    expand_weight,
    expand_bias,
    reduce_weight,
    reduce_bias,
    layer_scale,
):
    band = fields[0]
    cot = cotangent[0]
    rows, cols, channels = band.shape
    halves = channels // LANES
    hidden = expand_weight.shape[1]
    pitch = cols + 2 * LEAD
    wide = pitch + SUB
    ext = rows + 6
    cells = rows * cols
    faces, tiles = lax.axis_size("face"), lax.axis_size("tile")
    shape = jax.ShapeDtypeStruct
    strips = [shape((48, channels), BF16)] * 4
    sign = shape((SUB, LANES), F32)

    *rim_rows, columns = call(
        ends_kernel,
        [
            shape((3, cols, channels), BF16),
            shape((3, cols, channels), BF16),
            shape((rows, 32, channels), BF16),
        ],
        [],
        1_000_000_000,
        (band,),
    )
    beside = row_swap(*rim_rows)
    *sides, flags = call(
        edges_kernel,
        strips + [sign],
        [pltpu.VMEM((2, 16 * SUB, LANES), F32)],
        900_000_000,
        (columns, *beside, edge_match),
        smem=1,
    )
    got = glued_swap(sides)
    part, taps = call(
        own_rows_kernel,
        [
            pltpu.VMEM((halves * rows * (cols + SUB), LANES), F32),
            pltpu.VMEM((halves, 50, SUB, LANES), F32),
        ],
        [pltpu.VMEM((halves * ext * wide, LANES), F32)],
        4_500_000_000,
        (band, depth_kernel, depth_bias[None]),
        limit=4,
        after=(sides[0],),
    )
    part, taps = kept(part), kept(taps)
    result, pad, grad, mine, other, plain_near, plain_far, rim, vecs, bias_out = call(
        forward_kernel,
        [
            pltpu.HBM(band.shape, BF16),
            pltpu.HBM((halves * ext * wide, LANES), F32),
            pltpu.HBM((halves * rows * pitch + SUB, LANES), F32),
            shape((hidden, channels), F32),
            shape((hidden + 96, channels), BF16),
            shape((48, channels), BF16),
            shape((48, channels), BF16),
            pltpu.HBM((halves * 6 * (cols + SUB), LANES), F32),
            shape((8, channels), F32),
            shape((1, hidden), F32),
        ],
        [
            pltpu.VMEM((halves * 6 * (cols + SUB), LANES), F32),
            pltpu.VMEM(band.shape, BF16),
            pltpu.VMEM((halves * ext * wide, LANES), F32),
            pltpu.VMEM((halves * rows * pitch + SUB, LANES), F32),
            pltpu.VMEM((halves * rows * (cols + SUB), LANES), F32),
            pltpu.VMEM((cells, channels), BF16),
            pltpu.VMEM((cells, hidden), BF16),
            pltpu.VMEM((cells, hidden), BF16),
            pltpu.VMEM((cells, channels), BF16),
            pltpu.VMEM((2 * cols, channels), F32),
            pltpu.VMEM((12 * 32, LANES), F32),
            pltpu.SemaphoreType.DMA((4,)),
        ],
        12_000_000_000,
        (
            band, *beside, *got, cot, taps, norm_gain[None], norm_bias[None], reduce_bias[None],
            layer_scale[None], expand_bias.reshape(1, hidden), expand_weight, reduce_weight, part,
            flags,
        ),
        limit=20,
        left=(0, 1, 2, 7),
    )

    face_masks = list(range(faces - 1, 0, -1))
    chip_masks = list(range(2, tiles, 2))
    half, mirror = faces // 2, tiles - 2
    peer = swapped(other, "tile", 1)
    count = hidden // faces
    own, merged, *messages = call(
        lambda *refs: merge_kernel(face_masks, half, *refs),
        [shape((count, channels), F32), sign]
        + [shape((count + 48 * (m in (1, half)), channels), BF16) for m in face_masks],
        [],
        500_000_000,
        (mine, peer, plain_near, plain_far, flags),
    )

    def half_taps(h, after):
        return call(
            lambda *refs: taps_kernel(h, *refs),
            [shape((56, LANES), F32), sign],
            [],
            3_500_000_000 if h == 0 else 300_000_000,
            (grad, pad),
            after=after,
        )

    def half_inner(h, after):
        return call(
            lambda *refs: inner_kernel(h, *refs),
            [shape((rows * (cols + SUB), LANES), F32), sign],
            [],
            2_100_000_000 if h == 0 else 200_000_000,
            (grad, taps),
            after=after,
        )

    got = [swapped(v, "face", m) for v, m in zip(messages, face_masks)]
    rode = {m: got[face_masks.index(m)][count:] for m in (1, half)}
    inner0, token = half_inner(0, (merged,))
    taps0, token = half_taps(0, (token,))
    rows_z, rows_f = hidden // (faces * (tiles // 2)), hidden // faces
    got = got[::-1]
    part, dealt, *messages = call(
        lambda *refs: deal_kernel(chip_masks, mirror, 0, half - 1, *refs),
        [shape((rows_z, channels), F32), sign]
        + [shape((rows_z + 96 * (m == mirror), channels), BF16) for m in chip_masks],
        [pltpu.VMEM((rows_f, channels), F32)],
        100_000_000,
        (own, *got),
        after=(token,),
    )
    straight = rode
    got = [swapped(v, "tile", m) for v, m in zip(messages, chip_masks)]
    strips_got = got[chip_masks.index(mirror)]
    got = [g[96:] if m == mirror else g for g, m in zip(got, chip_masks)]
    columns = (straight[1], strips_got[0:48], straight[half], strips_got[48:96])
    taps1, _ = half_taps(1, (dealt,))
    (share,) = call(
        pack_shares_kernel,
        [shape((SMALL + rows_z, channels), BF16)],
        [pltpu.VMEM((SMALL, channels), F32)],
        1_000_000,
        (part, *got, taps0, taps1, bias_out, vecs),
    )
    got = gathered(share, "tile", chip_masks)
    within, across, token = call(
        rims_kernel,
        [shape((halves, 3, cols, LANES), BF16)] * 2 + [sign],
        [pltpu.VMEM((6 * cols, LANES), F32), pltpu.VMEM((16, LANES), F32)],
        900_000_000,
        (rim, *columns, flags),
    )
    arrived = row_swap(within, across)
    (pieces,) = call(
        pack_pieces_kernel,
        [shape((SMALL + rows_f, channels), BF16)],
        [],
        1_000_000,
        tuple(got),
        after=(token,),
    )
    got = gathered(pieces, "face", face_masks)
    inner1, _ = half_inner(1, (pieces,))
    grad_fields, token = call(
        fields_kernel,
        [shape(band.shape, BF16), sign],
        [pltpu.VMEM((cells, LANES), F32), pltpu.VMEM((16, LANES), F32)],
        200_000_000,
        (inner0, inner1, *arrived, *columns, cot, flags),
    )
    (pieces,) = call(
        pack_pieces_kernel,
        [shape((SMALL + hidden, channels), BF16)],
        [],
        1_000_000,
        tuple(got),
        after=(token,),
    )
    peer = swapped(pieces, "tile", 1)

    factor = 1.0 / math.sqrt(faces * tiles * cells)

    def finish(*refs):
        finish_kernel(factor, faces, tiles // 2, *refs)

    g_expand, g_reduce, g_taps, g_bias, g_vecs = call(
        finish,
        [
            shape((channels, hidden), F32),
            shape((hidden, channels), F32),
            shape((7, 7, channels), F32),
            shape((1, hidden), F32),
            shape((5, channels), F32),
        ],
        [],
        2_000_000_000,
        (pieces, peer),
    )
    return (
        result[None],
        grad_fields[None],
        g_taps,
        g_expand,
        g_reduce,
        g_bias.reshape(hidden),
        g_vecs,
    )


def solution(mesh):
    return jax.shard_map(
        shards,
        mesh=mesh,
        in_specs=(P("face", "tile"), P("face", "tile")) + (P(),) * 10,
        out_specs=(P("face", "tile"), P("face", "tile")) + (P(),) * 5,
        check_vma=False,
    )
```

```python
import math

import jax
import jax.numpy as jnp
from jax import lax
from jax.experimental import pallas as pl
from jax.experimental.pallas import tpu as pltpu
from jax.sharding import PartitionSpec as P

EPSILON = 1e-06
ROOT_COEF = 0.7978845608028654
CUBIC_COEF = 0.044715
LANES = 128
SUB = 8
LEAD = 8
SMALL = 64
F32 = jnp.float32
BF16 = jnp.bfloat16


def dot(a, b, dims):
    return lax.dot_general(a, b, (dims, ((), ())), preferred_element_type=F32)


def call(body, outs, scratch, flops, args, smem=0, after=(), limit=4, left=()):
    vmem = pl.BlockSpec(memory_space=pltpu.VMEM)
    scalar = pl.BlockSpec(memory_space=pltpu.SMEM)
    anywhere = pl.BlockSpec(memory_space=pl.ANY)
    outside = pl.BlockSpec(memory_space=pltpu.HBM)
    count = len(args)

    def run(*refs):
        body(*refs[:count], *refs[count + len(after) :])

    return pl.pallas_call(
        run,
        out_shape=outs,
        in_specs=[vmem] * (count - smem) + [scalar] * smem + [anywhere] * len(after),
        out_specs=[outside if i in left else vmem for i in range(len(outs))],
        scratch_shapes=scratch,
        compiler_params=pltpu.CompilerParams(vmem_limit_bytes=limit * 1024 * 1024),
        cost_estimate=pl.CostEstimate(flops=flops, bytes_accessed=1 << 20, transcendentals=0),
    )(*args, *after)


def kept(x):
    return pltpu.with_memory_space_constraint(x, pltpu.VMEM)


def strided(ref, start, groups):
    return ref[pl.ds(start, SUB, stride=groups), :]


def gluing(match, flags):
    face = lax.axis_index("face")
    near = jnp.where(match[face, 0, 0] == face ^ 1, 0, 1)
    flags[...] = jnp.zeros_like(flags)
    for k, value in enumerate((near, match[face, near, 2], match[face, 1 - near, 2])):
        flags[k : k + 1, :] = jnp.full((1, LANES), value, jnp.int32).astype(F32)


def glued(flags):
    return flags[0:1, :] == 0.0, flags[1:2, :] == 1.0, flags[2:3, :] == 1.0


def pack_columns(tile, count, first, held, outs):
    vals = {}
    for side in range(2):
        for h in range(2):
            held[...] = jnp.zeros_like(held)
            for i in range(count):
                t = tile(side, h, i)
                held[0, i * SUB : (i + 1) * SUB, :] = t
                held[1, (count - 1 - i) * SUB : (count - i) * SUB, :] = t
            for v in range(2):
                for d in range(3):
                    vals[side, h, v, d] = held[v, pl.ds(tile.column(side, d), 16, stride=SUB), :]
    for h in range(2):
        lane = slice(h * LANES, (h + 1) * LANES)
        for v in range(2):
            for d in range(3):
                west, east = vals[0, h, v, d], vals[1, h, v, d]
                at = slice(d * 16, d * 16 + 16)
                outs[v][at, lane] = jnp.where(first, west, east).astype(BF16)
                outs[2 + v][at, lane] = jnp.where(first, east, west).astype(BF16)


def unpack_columns(first, turn_near, turn_far, got):
    def value(side, h, d):
        lane = slice(h * LANES, (h + 1) * LANES)
        parts = [g[d * 16 : d * 16 + 16, lane].astype(F32) for g in got]
        one = jnp.where(turn_near, parts[1], parts[0])
        two = jnp.where(turn_far, parts[3], parts[2])
        return jnp.where(first, one, two) if side == 0 else jnp.where(first, two, one)

    return value


def ends_kernel(band, within, across, columns):
    rows, cols, _ = band.shape
    even = (lax.axis_index("tile") & 1) == 0
    for k in range(3):
        top, bottom = band[k], band[rows - 3 + k]
        within[k] = jnp.where(even, bottom, top)
        across[k] = jnp.where(even, top, bottom)
    for r in range(rows):
        columns[r, 0:16, :] = band[r, 0:16, :]
        columns[r, 16:32, :] = band[r, cols - 16 : cols, :]


def edges_kernel(columns, within, across, match, *refs):
    outs, flags, held = refs[:4], refs[4], refs[5]
    gluing(match, flags)
    up, down = above_below(within, across)
    rows, _, _ = columns.shape
    _, cols, _ = within.shape
    first, _, _ = glued(flags)

    def tile(side, h, i):
        lane = slice(h * LANES, (h + 1) * LANES)
        at = slice(0, 16) if side == 0 else slice(cols - 16, cols)
        if i < 3:
            v = up(i, at, lane)
        elif i < rows + 3:
            v = columns[i - 3, slice(0, 16) if side == 0 else slice(16, 32), lane]
        else:
            v = down(i - rows - 3, at, lane)
        return v.astype(F32)[0:SUB] if side == 0 else v.astype(F32)[SUB:16]

    tile.column = lambda side, d: d if side == 0 else SUB - 1 - d
    pack_columns(tile, rows + 6, first, held, outs)


def fill_pad(pad, halves, ext, wide, cols, source, which):
    for h in range(halves):
        lane = slice(h * LANES, (h + 1) * LANES)
        for i in which:
            at = (h * ext + i) * wide
            pad[at : at + LEAD, :] = jnp.zeros((LEAD, LANES), F32)
            pad[at + LEAD : at + LEAD + cols, :] = source(i, lane).astype(F32)
            pad[at + LEAD + cols : at + wide, :] = jnp.zeros((LEAD + SUB, LANES), F32)


def own_rows_kernel(band, kernel, bias, conv, taps, pad):
    for h in range(2):
        lane = slice(h * LANES, (h + 1) * LANES)
        for a in range(7):
            row = kernel[a].astype(F32)
            for b in range(7):
                taps[h, a * 7 + b] = jnp.broadcast_to(row[b : b + 1, lane], (SUB, LANES))
        taps[h, 49] = jnp.broadcast_to(bias[:, lane], (SUB, LANES))
    rows, cols, channels = band.shape
    halves = channels // LANES
    pitch = cols + 2 * LEAD
    wide = pitch + SUB
    ext = rows + 6
    groups = cols // SUB + 1
    cpitch = groups * SUB
    fill_pad(pad, halves, ext, wide, cols, lambda i, lane: band[i - 3, :, lane], range(3, rows + 3))

    def half(h, carry):
        for r in range(rows):
            acc = [taps[h, 49]] * groups
            for a in range(7):
                if not 3 <= r + a < rows + 3:
                    continue
                base = (h * ext + r + a) * wide + LEAD - 3
                tap = [taps[h, a * 7 + b] for b in range(7)]
                for jj in range(groups + 6):
                    x = strided(pad, base + jj, groups)
                    for b in range(7):
                        if 0 <= jj - b < groups:
                            acc[jj - b] = acc[jj - b] + tap[b] * x
            for j in range(groups):
                conv[pl.ds((h * rows + r) * cpitch + j, SUB, stride=groups), :] = acc[j]
        return carry

    lax.fori_loop(0, halves, half, 0)


def forward_kernel(
    band, within, across, got0, got1, got2, got3, cot, taps, gain, shift, bias2, scale, bias1, w1, w2, part, flags,
    result_out, pad_out, grad_out, mine, other, plain_near, plain_far, vecs, bias_out,
    result, pad, grad, conv, normed, act, pre, gbr, tmp, strip, sems,
):
    rows, cols, channels = band.shape
    halves = channels // LANES
    pitch = cols + 2 * LEAD
    wide = pitch + SUB
    ext = rows + 6
    groups = cols // SUB + 1
    cpitch = groups * SUB
    hidden = w1.shape[1]

    first, turn_near, turn_far = glued(flags)
    arrived = unpack_columns(first, turn_near, turn_far, (got0, got1, got2, got3))

    up, down = above_below(within, across)

    def source(i, lane):
        if i < 3:
            return up(i, slice(None), lane)
        return band[i - 3, :, lane] if i < rows + 3 else down(i - rows - 3, slice(None), lane)

    fill_pad(pad, halves, ext, wide, cols, source, range(ext))
    for h in range(halves):
        for d in range(3):
            for side in range(2):
                col = LEAD - 1 - d if side == 0 else LEAD + cols + d
                v = arrived(side, h, d)
                at = h * ext * wide + col
                pad[pl.ds(at, SUB, stride=wide), :] = v[0:SUB]
                pad[pl.ds(at + SUB * wide, ext - SUB, stride=wide), :] = v[SUB:ext]
        for r in range(rows):
            at = (h * rows + r) * pitch
            grad[at : at + LEAD, :] = jnp.zeros((LEAD, LANES), F32)
            grad[at + LEAD + cols : at + pitch, :] = jnp.zeros((LEAD, LANES), F32)

    keep_pad = pltpu.make_async_copy(pad, pad_out, sems.at[0])
    keep_pad.start()
    tail = halves * rows * pitch
    grad[tail : tail + SUB, :] = jnp.zeros((SUB, LANES), F32)

    where = lax.broadcasted_iota(jnp.int32, (SUB, LANES), 0)
    at_west, at_east = where == 0, where == SUB - 1
    none = jnp.zeros((SUB, LANES), F32)
    over = cols + 3 - (SUB - 1) * groups

    def complete(h, carry):
        for r in range(rows):
            acc = [strided(part, (h * rows + r) * cpitch + j, groups) for j in range(groups)]
            for a in range(7):
                base = (h * ext + r + a) * wide + LEAD - 3
                tap = [taps[h, a * 7 + b] for b in range(7)]
                if not 3 <= r + a < rows + 3:
                    for jj in range(groups + 6):
                        x = strided(pad, base + jj, groups)
                        for b in range(7):
                            if 0 <= jj - b < groups:
                                acc[jj - b] = acc[jj - b] + tap[b] * x
                    continue
                for d in range(3):
                    x = jnp.where(at_west, strided(pad, base + d, groups), none)
                    for b in range(d + 1):
                        acc[d - b] = acc[d - b] + tap[b] * x
                    x = jnp.where(at_east, strided(pad, base + over + d, groups), none)
                    for b in range(4 + d, 7):
                        acc[over + d - b] = acc[over + d - b] + tap[b] * x
            for j in range(groups):
                conv[pl.ds((h * rows + r) * cpitch + j, SUB, stride=groups), :] = acc[j]
        return carry

    lax.fori_loop(0, halves, complete, 0)

    step = 2 * cols
    gain, shift, bias2, scale = gain[...], shift[...], bias2[...], scale[...]
    tiles = hidden // 256

    def chunk(m, carry):
        s_conv, s_gain, s_norm, s_cot, s_scale = carry
        at = pl.multiple_of(m * step, step)
        x = jnp.concatenate(
            [
                jnp.concatenate(
                    [
                        conv[pl.ds(pl.multiple_of((h * rows + 2 * m + k) * cpitch, 8), cols), :]
                        for k in range(2)
                    ],
                    axis=0,
                )
                for h in range(halves)
            ],
            axis=1,
        )
        centred = x - jnp.mean(x, axis=-1, keepdims=True)
        inverse = lax.rsqrt(jnp.mean(centred * centred, axis=-1, keepdims=True) + EPSILON)
        standard = centred * inverse
        lane_in = (standard * gain + shift).astype(BF16)
        normed[pl.ds(at, step), :] = lane_in
        tmp[...] = standard
        upstream = cot[pl.ds(2 * m, 2)].reshape(step, channels).astype(F32)
        g_branch = (upstream * scale).astype(BF16)
        gbr[pl.ds(at, step), :] = g_branch
        for n in range(tiles):
            hid = slice(n * 256, (n + 1) * 256)
            v = dot(lane_in, w1[:, hid], ((1,), (0,))) + bias1[:, hid]
            v2 = v * v
            half = 0.5 + 0.5 * jnp.tanh(v * (ROOT_COEF + ROOT_COEF * CUBIC_COEF * v2))
            act[pl.ds(at, step), hid] = (v * half).astype(BF16)
            slope = half * (
                1.0 + (1.0 - half) * (v * (2 * ROOT_COEF + 6 * ROOT_COEF * CUBIC_COEF * v2))
            )
            d_act = dot(g_branch, w2[hid, :], ((1,), (1,)))
            g_pre = (d_act * slope).astype(BF16)
            pre[pl.ds(at, step), hid] = g_pre
            bias_out[:, hid] += jnp.sum(g_pre.astype(F32), axis=0, keepdims=True)
        branch = dot(act[pl.ds(at, step), :], w2[...], ((1,), (0,))) + bias2
        residual = band[pl.ds(2 * m, 2)].reshape(step, channels).astype(F32)
        result[pl.ds(2 * m, 2)] = (
            (residual + scale * branch).astype(BF16).reshape(2, cols, channels)
        )
        s_cot = s_cot + jnp.sum(upstream, axis=0, keepdims=True)
        s_scale = s_scale + jnp.sum(upstream * branch, axis=0, keepdims=True)
        g_norm = dot(pre[pl.ds(at, step), :], w1[...], ((1,), (1,)))
        standard = tmp[...]
        u = g_norm * gain
        g_conv = (
            u
            - jnp.mean(u, axis=-1, keepdims=True)
            - standard * jnp.mean(u * standard, axis=-1, keepdims=True)
        ) * inverse
        for h in range(halves):
            for k in range(2):
                dst = (h * rows + 2 * m + k) * pitch + LEAD
                grad[pl.ds(pl.multiple_of(dst, 8), cols), :] = g_conv[
                    k * cols : (k + 1) * cols, h * LANES : (h + 1) * LANES
                ]
        s_conv = s_conv + jnp.sum(g_conv, axis=0, keepdims=True)
        s_gain = s_gain + jnp.sum(g_norm * standard, axis=0, keepdims=True)
        s_norm = s_norm + jnp.sum(g_norm, axis=0, keepdims=True)
        return (s_conv, s_gain, s_norm, s_cot, s_scale)

    bias_out[...] = jnp.zeros_like(bias_out)
    zero = jnp.zeros((1, channels), F32)
    sums = lax.fori_loop(0, rows // 2, chunk, (zero,) * 5, unroll=True)
    sums = (sums[0], sums[1], sums[2], sums[3] * scale, sums[4])
    vecs[...] = jnp.concatenate(list(sums) + [zero] * 3, axis=0)

    keep_grad = pltpu.make_async_copy(grad, grad_out, sems.at[1])
    keep_grad.start()
    keep_result = pltpu.make_async_copy(result, result_out, sems.at[2])
    keep_result.start()

    strip[...] = jnp.zeros_like(strip)
    for h in range(halves):
        lane = slice(h * LANES, (h + 1) * LANES)

        def column(c, h=h):
            return grad[pl.ds(h * rows * pitch + LEAD + c, SUB, stride=pitch), :]

        for side in range(2):
            edge = [column(c if side == 0 else cols - 1 - c) for c in range(3)]
            for d in range(3):
                slot = ((side * 3 + d) * halves + h) * 32
                for a in range(7):
                    total = none
                    for c in range(3 - d):
                        b = 2 - d - c if side == 0 else 4 + d + c
                        total = total + taps[h, a * 7 + b] * edge[c]
                    strip[slot + a : slot + a + SUB, :] += total
                for o in range(ext):
                    strip[slot + 16 + o : slot + 17 + o, :] = strip[
                        slot + ext - 1 - o : slot + ext - o, :
                    ]
        for d in range(3):
            slots = [((side * 3 + d) * halves + h) * 32 for side in range(2)]
            for turned in range(2):
                west, east = [strip[k + 16 * turned : k + 16 * turned + 16, :] for k in slots]
                one = jnp.where(first, west, east).astype(BF16)
                two = jnp.where(first, east, west).astype(BF16)
                if turned:
                    other[hidden + 16 * d : hidden + 16 * d + 16, lane] = one
                    other[hidden + 48 + 16 * d : hidden + 64 + 16 * d, lane] = two
                else:
                    plain_near[16 * d : 16 * d + 16, lane] = one
                    plain_far[16 * d : 16 * d + 16, lane] = two

    even = (lax.axis_index("tile") & 1) == 0
    for n in range(tiles):
        hid = slice(n * 256, (n + 1) * 256)
        g_expand = dot(normed[...], pre[:, hid], ((0,), (0,)))
        g_reduce = dot(act[:, hid], gbr[...], ((0,), (0,)))
        mine[hid, :] = jnp.where(even, g_expand, g_reduce)
        other[hid, :] = jnp.where(even, g_reduce, g_expand).astype(BF16)
    keep_pad.wait()
    keep_grad.wait()
    keep_result.wait()


def spread_row(grad, taps, h, o, rows, pitch, groups):
    acc = [jnp.zeros((SUB, LANES), F32)] * groups
    for a in range(7):
        if not 0 <= o - a < rows:
            continue
        src = (h * rows + o - a) * pitch + LEAD + 3
        tap = [taps[h, a * 7 + b] for b in range(7)]
        for jj in range(-6, groups):
            x = strided(grad, src + jj, groups)
            for b in range(7):
                if 0 <= jj + b < groups:
                    acc[jj + b] = acc[jj + b] + tap[b] * x
    return acc


def inner_kernel(h, grad, taps, out, token):
    token[...] = jnp.zeros_like(token)
    rows = 8
    cpitch = out.shape[0] // rows
    pitch = cpitch + LEAD
    groups = cpitch // SUB
    for r in range(rows):
        acc = spread_row(grad, taps, h, r + 3, rows, pitch, groups)
        for j in range(groups):
            out[pl.ds(r * cpitch + j, SUB, stride=groups), :] = acc[j]


def taps_kernel(h, grad, pad, out, token):
    token[...] = jnp.zeros_like(token)
    halves, rows = 2, 8
    ext = rows + 6
    pitch = (grad.shape[0] - SUB) // (halves * rows)
    wide = pad.shape[0] // (halves * ext)
    cols = pitch - 2 * LEAD
    groups = cols // SUB + 1

    def some(first, count):
        acc = [[jnp.zeros((SUB, LANES), F32)] * 7 for _ in range(count)]
        for i in range(rows + count - 1):
            base = (h * ext + i + first) * wide + LEAD - 3
            use = [k for k in range(count) if 0 <= i - k < rows]
            g = {}
            for jj in range(groups + 6):
                if jj < groups:
                    for k in use:
                        at = (h * rows + i - k) * pitch + LEAD + jj
                        g[k, jj] = strided(grad, at, groups)
                x = strided(pad, base + jj, groups)
                for b in range(7):
                    j = jj - b
                    if 0 <= j < groups:
                        for k in use:
                            acc[k][b] = acc[k][b] + g[k, j] * x
        for k in range(count):
            for b in range(7):
                out[pl.ds((first + k) * 7 + b, 1), :] = jnp.sum(acc[k][b], axis=0, keepdims=True)

    def pair(p, carry):
        some(2 * p, 2)
        return carry

    lax.fori_loop(0, 3, pair, 0)
    some(6, 1)


def rims_kernel(grad, taps, got0, got1, got2, got3, flags, within, across, token, total, held):
    token[...] = jnp.zeros_like(token)
    halves, _, cols, _ = within.shape
    even = (lax.axis_index("tile") & 1) == 0
    rows = 8
    pitch = cols + 2 * LEAD
    groups = cols // SUB + 1
    cpitch = groups * SUB
    first, turn_near, turn_far = glued(flags)
    arrived = unpack_columns(first, turn_near, turn_far, (got0, got1, got2, got3))
    for h in range(halves):
        for k in range(6):
            acc = spread_row(grad, taps, h, k if k < 3 else rows + k, rows, pitch, groups)
            for j in range(groups):
                total[pl.ds(k * cpitch + j, SUB, stride=groups), :] = acc[j]
        for side in range(2):
            for d in range(3):
                held[...] = arrived(side, h, d)
                for k in range(6):
                    o = k if k < 3 else k + 8
                    at = k * cpitch + (d if side == 0 else cols - 1 - d)
                    total[at : at + 1, :] += held[o : o + 1, :]
        for k in range(3):
            top = total[k * cpitch : k * cpitch + cols, :].astype(BF16)
            bottom = total[(k + 3) * cpitch : (k + 3) * cpitch + cols, :].astype(BF16)
            within[h, k] = jnp.where(even, bottom, top)
            across[h, k] = jnp.where(even, top, bottom)


def fields_kernel(inner0, inner1, within, across, got0, got1, got2, got3, cot, flags, out, token, total, held):
    token[...] = jnp.zeros_like(token)
    rows, cols, channels = cot.shape
    halves = channels // LANES
    cpitch = inner0.shape[0] // rows
    from_up, from_down = above_below(within, across)
    first, turn_near, turn_far = glued(flags)
    arrived = unpack_columns(first, turn_near, turn_far, (got0, got1, got2, got3))
    for h in range(halves):
        lane = slice(h * LANES, (h + 1) * LANES)
        for r in range(rows):
            at = r * cpitch
            own = (inner0, inner1)[h][at : at + cols, :] + cot[r, :, lane].astype(F32)
            if r < 3:
                own = own + from_up(h, r).astype(F32)
            if r >= rows - 3:
                own = own + from_down(h, r - rows + 3).astype(F32)
            total[r * cols : (r + 1) * cols, :] = own
        for side in range(2):
            for d in range(3):
                held[...] = arrived(side, h, d)
                at = pl.ds(d if side == 0 else cols - 1 - d, SUB, stride=cols)
                total[at, :] = total[at, :] + held[3 : 3 + rows, :]
        for r in range(rows):
            out[r, :, lane] = total[r * cols : (r + 1) * cols, :].astype(BF16)


def merge_kernel(masks, half, mine, peer, plain_near, plain_far, flags, own, token, *messages):
    _, turn_near, turn_far = glued(flags)
    token[...] = jnp.zeros_like(token)
    hidden = mine.shape[0]
    count = own.shape[0]
    face = lax.axis_index("face")

    def share(mask):
        at = pl.ds(pl.multiple_of((face ^ mask) * count, count), count)
        return mine[at, :] + peer[at, :].astype(F32)

    def choose(turn, at, plain, message):
        for h in range(2):
            lane = slice(h * LANES, (h + 1) * LANES)
            turned = peer[at : at + 48, lane].astype(F32)
            message[count : count + 48, lane] = jnp.where(
                turn, turned, plain[:, lane].astype(F32)
            ).astype(BF16)

    own[...] = share(0)
    for mask, message in zip(masks, messages):
        message[0:count, :] = share(mask).astype(BF16)
        if mask == 1:
            choose(turn_near, hidden, plain_near, message)
        if mask == half:
            choose(turn_far, hidden + 48, plain_far, message)


def deal_kernel(masks, mirror, near, far, own, *refs):
    count = own.shape[0]
    got, (part, token, *messages), total = refs[: len(refs) - 3 - len(masks)], refs[
        len(refs) - 3 - len(masks) : -1
    ], refs[-1]
    token[...] = jnp.zeros_like(token)
    size = part.shape[0]
    chip = lax.axis_index("tile") >> 1
    total[...] = tree_sum([own[...]] + [g[0:count, :] for g in got])

    def share(place):
        return total[pl.ds(pl.multiple_of(place * size, size), size), :]

    part[...] = share(chip)
    for mask, message in zip(masks, messages):
        at = 0
        if mask == mirror:
            message[0:48, :] = got[near][count:, :]
            message[48:96, :] = got[far][count:, :]
            at = 96
        message[at : at + size, :] = share(chip ^ (mask >> 1)).astype(BF16)


def pack_shares_kernel(own, *refs):
    *got, taps0, taps1, bias, vecs, out, held = refs
    count, channels = own.shape
    held[...] = jnp.zeros_like(held)
    held[0:49, 0:LANES] = taps0[0:49, :]
    held[0:49, LANES : 2 * LANES] = taps1[0:49, :]
    parts = bias.shape[1] // channels
    for n in range(parts):
        held[49 + n : 50 + n, :] = bias[:, n * channels : (n + 1) * channels]
    held[49 + parts : 54 + parts, :] = vecs[0:5, :]
    out[0:SMALL, :] = held[...].astype(BF16)
    out[SMALL:, :] = tree_sum([own[...]] + [g[0:count, :] for g in got]).astype(BF16)


def pack_pieces_kernel(own, *refs):
    *got, out = refs
    parts = [own[...].astype(F32)] + [g[...].astype(F32) for g in got]
    out[0:SMALL, :] = tree_sum([p[0:SMALL] for p in parts]).astype(BF16)
    out[SMALL:, :] = jnp.concatenate([p[SMALL:] for p in parts], 0).astype(BF16)


def finish_kernel(factor, faces, chips, mine, peer, expand, reduce, g_taps, g_bias, vecs):
    hidden, channels = reduce.shape
    count = hidden // (faces * chips)
    face = lax.axis_index("face")
    chip = lax.axis_index("tile") >> 1
    even = (lax.axis_index("tile") & 1) == 0
    small = mine[0:SMALL, :].astype(F32) + peer[0:SMALL, :].astype(F32)
    small = small * factor
    for f in range(faces):
        for z in range(chips):
            at = SMALL + (f * chips + z) * count
            own = mine[at : at + count, :].astype(F32) * factor
            got = peer[at : at + count, :].astype(F32) * factor
            to = ((face ^ f) * chips + (chip ^ z)) * count
            reduce[pl.ds(pl.multiple_of(to, count), count), :] = jnp.where(even, got, own)
            row = pl.multiple_of(lax.rem(to, channels), count)
            col = pl.multiple_of((to // channels) * channels, channels)
            expand[pl.ds(row, count), pl.ds(col, channels)] = jnp.where(even, own, got)
    for a in range(7):
        g_taps[a] = small[a * 7 : a * 7 + 7, :]
    for n in range(hidden // channels):
        g_bias[:, n * channels : (n + 1) * channels] = small[49 + n : 50 + n, :]
    first = 49 + hidden // channels
    vecs[...] = small[first : first + 5, :]


def face_swap(x, mask, turned=False):
    faces, tiles = lax.axis_size("face"), lax.axis_size("tile")
    pairs = [
        (f * tiles + t, (f ^ mask) * tiles + (tiles - 1 - t if turned else t))
        for f in range(faces)
        for t in range(tiles)
    ]
    return lax.ppermute(x, ("face", "tile"), pairs)


def glued_swap(strips):
    near_plain, near_turned, far_plain, far_turned = strips
    half = lax.axis_size("face") // 2
    return (
        face_swap(near_plain, 1),
        face_swap(near_turned, 1, True),
        face_swap(far_plain, half),
        face_swap(far_turned, half, True),
    )


def row_swap(within, across):
    count = lax.axis_size("tile")
    pairs = [(i, i + 1) for i in range(1, count - 1, 2)]
    return (
        swapped(within, "tile", 1),
        lax.ppermute(across, "tile", pairs + [(j, i) for i, j in pairs]),
    )


def above_below(within, across):
    even = (lax.axis_index("tile") & 1) == 0

    def up(*at):
        return jnp.where(even, across[at], within[at])

    def down(*at):
        return jnp.where(even, within[at], across[at])

    return up, down


def swapped(x, axis, mask):
    return lax.ppermute(x, axis, [(i, i ^ mask) for i in range(lax.axis_size(axis))])


def tree_sum(parts):
    parts = [p.astype(F32) for p in parts]
    while len(parts) > 1:
        parts = [parts[i] + parts[i + 1] for i in range(0, len(parts), 2)]
    return parts[0]


def gathered(x, axis, masks):
    got = [swapped(x, axis, m) for m in masks]
    return [x] + [got[masks.index(m)] for m in sorted(masks)]


def shards(
    fields,
    cotangent,
    edge_match,
    depth_kernel,
    depth_bias,
    norm_gain,
    norm_bias,
    expand_weight,
    expand_bias,
    reduce_weight,
    reduce_bias,
    layer_scale,
):
    band = fields[0]
    cot = cotangent[0]
    rows, cols, channels = band.shape
    halves = channels // LANES
    hidden = expand_weight.shape[1]
    pitch = cols + 2 * LEAD
    wide = pitch + SUB
    ext = rows + 6
    cells = rows * cols
    faces, tiles = lax.axis_size("face"), lax.axis_size("tile")
    shape = jax.ShapeDtypeStruct
    strips = [shape((48, channels), BF16)] * 4
    sign = shape((SUB, LANES), F32)

    *rim_rows, columns = call(
        ends_kernel,
        [
            shape((3, cols, channels), BF16),
            shape((3, cols, channels), BF16),
            shape((rows, 32, channels), BF16),
        ],
        [],
        1_000_000_000,
        (band,),
    )
    beside = row_swap(*rim_rows)
    *sides, flags = call(
        edges_kernel,
        strips + [sign],
        [pltpu.VMEM((2, 16 * SUB, LANES), F32)],
        900_000_000,
        (columns, *beside, edge_match),
        smem=1,
    )
    got = glued_swap(sides)
    part, taps = call(
        own_rows_kernel,
        [
            pltpu.VMEM((halves * rows * (cols + SUB), LANES), F32),
            pltpu.VMEM((halves, 50, SUB, LANES), F32),
        ],
        [pltpu.VMEM((halves * ext * wide, LANES), F32)],
        4_500_000_000,
        (band, depth_kernel, depth_bias[None]),
        limit=4,
        after=(sides[0],),
    )
    part, taps = kept(part), kept(taps)
    result, pad, grad, mine, other, plain_near, plain_far, vecs, bias_out = call(
        forward_kernel,
        [
            pltpu.HBM(band.shape, BF16),
            pltpu.HBM((halves * ext * wide, LANES), F32),
            pltpu.HBM((halves * rows * pitch + SUB, LANES), F32),
            shape((hidden, channels), F32),
            shape((hidden + 96, channels), BF16),
            shape((48, channels), BF16),
            shape((48, channels), BF16),
            shape((8, channels), F32),
            shape((1, hidden), F32),
        ],
        [
            pltpu.VMEM(band.shape, BF16),
            pltpu.VMEM((halves * ext * wide, LANES), F32),
            pltpu.VMEM((halves * rows * pitch + SUB, LANES), F32),
            pltpu.VMEM((halves * rows * (cols + SUB), LANES), F32),
            pltpu.VMEM((cells, channels), BF16),
            pltpu.VMEM((cells, hidden), BF16),
            pltpu.VMEM((cells, hidden), BF16),
            pltpu.VMEM((cells, channels), BF16),
            pltpu.VMEM((2 * cols, channels), F32),
            pltpu.VMEM((12 * 32, LANES), F32),
            pltpu.SemaphoreType.DMA((3,)),
        ],
        12_000_000_000,
        (
            band, *beside, *got, cot, taps, norm_gain[None], norm_bias[None], reduce_bias[None],
            layer_scale[None], expand_bias.reshape(1, hidden), expand_weight, reduce_weight, part,
            flags,
        ),
        limit=20,
        left=(0, 1, 2),
    )

    face_masks = list(range(faces - 1, 0, -1))
    chip_masks = list(range(2, tiles, 2))
    half, mirror = faces // 2, tiles - 2
    peer = swapped(other, "tile", 1)
    count = hidden // faces
    own, merged, *messages = call(
        lambda *refs: merge_kernel(face_masks, half, *refs),
        [shape((count, channels), F32), sign]
        + [shape((count + 48 * (m in (1, half)), channels), BF16) for m in face_masks],
        [],
        500_000_000,
        (mine, peer, plain_near, plain_far, flags),
    )

    def half_taps(h, after):
        return call(
            lambda *refs: taps_kernel(h, *refs),
            [shape((56, LANES), F32), sign],
            [],
            3_500_000_000 if h == 0 else 300_000_000,
            (grad, pad),
            after=after,
        )

    def half_inner(h, after):
        return call(
            lambda *refs: inner_kernel(h, *refs),
            [shape((rows * (cols + SUB), LANES), F32), sign],
            [],
            2_100_000_000 if h == 0 else 200_000_000,
            (grad, taps),
            after=after,
        )

    got = [swapped(v, "face", m) for v, m in zip(messages, face_masks)]
    rode = {m: got[face_masks.index(m)][count:] for m in (1, half)}
    inner0, token = half_inner(0, (merged,))
    taps0, token = half_taps(0, (token,))
    rows_z, rows_f = hidden // (faces * (tiles // 2)), hidden // faces
    got = got[::-1]
    part, dealt, *messages = call(
        lambda *refs: deal_kernel(chip_masks, mirror, 0, half - 1, *refs),
        [shape((rows_z, channels), F32), sign]
        + [shape((rows_z + 96 * (m == mirror), channels), BF16) for m in chip_masks],
        [pltpu.VMEM((rows_f, channels), F32)],
        100_000_000,
        (own, *got),
        after=(token,),
    )
    straight = rode
    got = [swapped(v, "tile", m) for v, m in zip(messages, chip_masks)]
    strips_got = got[chip_masks.index(mirror)]
    got = [g[96:] if m == mirror else g for g, m in zip(got, chip_masks)]
    columns = (straight[1], strips_got[0:48], straight[half], strips_got[48:96])
    taps1, _ = half_taps(1, (dealt,))
    (share,) = call(
        pack_shares_kernel,
        [shape((SMALL + rows_z, channels), BF16)],
        [pltpu.VMEM((SMALL, channels), F32)],
        1_000_000,
        (part, *got, taps0, taps1, bias_out, vecs),
    )
    got = gathered(share, "tile", chip_masks)
    within, across, token = call(
        rims_kernel,
        [shape((halves, 3, cols, LANES), BF16)] * 2 + [sign],
        [pltpu.VMEM((6 * (cols + SUB), LANES), F32), pltpu.VMEM((16, LANES), F32)],
        900_000_000,
        (grad, taps, *columns, flags),
    )
    arrived = row_swap(within, across)
    (pieces,) = call(
        pack_pieces_kernel,
        [shape((SMALL + rows_f, channels), BF16)],
        [],
        1_000_000,
        tuple(got),
        after=(token,),
    )
    got = gathered(pieces, "face", face_masks)
    inner1, _ = half_inner(1, (pieces,))
    grad_fields, token = call(
        fields_kernel,
        [shape(band.shape, BF16), sign],
        [pltpu.VMEM((cells, LANES), F32), pltpu.VMEM((16, LANES), F32)],
        200_000_000,
        (inner0, inner1, *arrived, *columns, cot, flags),
    )
    (pieces,) = call(
        pack_pieces_kernel,
        [shape((SMALL + hidden, channels), BF16)],
        [],
        1_000_000,
        tuple(got),
        after=(token,),
    )
    peer = swapped(pieces, "tile", 1)

    factor = 1.0 / math.sqrt(faces * tiles * cells)

    def finish(*refs):
        finish_kernel(factor, faces, tiles // 2, *refs)

    g_expand, g_reduce, g_taps, g_bias, g_vecs = call(
        finish,
        [
            shape((channels, hidden), F32),
            shape((hidden, channels), F32),
            shape((7, 7, channels), F32),
            shape((1, hidden), F32),
            shape((5, channels), F32),
        ],
        [],
        2_000_000_000,
        (pieces, peer),
    )
    return (
        result[None],
        grad_fields[None],
        g_taps,
        g_expand,
        g_reduce,
        g_bias.reshape(hidden),
        g_vecs,
    )


def solution(mesh):
    return jax.shard_map(
        shards,
        mesh=mesh,
        in_specs=(P("face", "tile"), P("face", "tile")) + (P(),) * 10,
        out_specs=(P("face", "tile"), P("face", "tile")) + (P(),) * 5,
        check_vma=False,
    )
```

```python
import math

import jax
import jax.numpy as jnp
from jax import lax
from jax.experimental import pallas as pl
from jax.experimental.pallas import tpu as pltpu
from jax.sharding import PartitionSpec as P

EPSILON = 1e-06
ROOT_COEF = 0.7978845608028654
CUBIC_COEF = 0.044715
LANES = 128
SUB = 8
LEAD = 8
SMALL = 64
F32 = jnp.float32
BF16 = jnp.bfloat16


def dot(a, b, dims):
    return lax.dot_general(a, b, (dims, ((), ())), preferred_element_type=F32)


def call(body, outs, scratch, flops, args, smem=0, after=(), limit=4, left=()):
    vmem = pl.BlockSpec(memory_space=pltpu.VMEM)
    scalar = pl.BlockSpec(memory_space=pltpu.SMEM)
    anywhere = pl.BlockSpec(memory_space=pl.ANY)
    outside = pl.BlockSpec(memory_space=pltpu.HBM)
    count = len(args)

    def run(*refs):
        body(*refs[:count], *refs[count + len(after) :])

    return pl.pallas_call(
        run,
        out_shape=outs,
        in_specs=[vmem] * (count - smem) + [scalar] * smem + [anywhere] * len(after),
        out_specs=[outside if i in left else vmem for i in range(len(outs))],
        scratch_shapes=scratch,
        compiler_params=pltpu.CompilerParams(vmem_limit_bytes=limit * 1024 * 1024),
        cost_estimate=pl.CostEstimate(flops=flops, bytes_accessed=1 << 20, transcendentals=0),
    )(*args, *after)


def kept(x):
    return pltpu.with_memory_space_constraint(x, pltpu.VMEM)


def strided(ref, start, groups):
    return ref[pl.ds(start, SUB, stride=groups), :]


def gluing(match, flags):
    face = lax.axis_index("face")
    near = jnp.where(match[face, 0, 0] == face ^ 1, 0, 1)
    flags[...] = jnp.zeros_like(flags)
    for k, value in enumerate((near, match[face, near, 2], match[face, 1 - near, 2])):
        flags[k : k + 1, :] = jnp.full((1, LANES), value, jnp.int32).astype(F32)


def glued(flags):
    return flags[0:1, :] == 0.0, flags[1:2, :] == 1.0, flags[2:3, :] == 1.0


def pack_columns(tile, count, first, held, outs):
    vals = {}
    for side in range(2):
        for h in range(2):
            held[...] = jnp.zeros_like(held)
            for i in range(count):
                t = tile(side, h, i)
                held[0, i * SUB : (i + 1) * SUB, :] = t
                held[1, (count - 1 - i) * SUB : (count - i) * SUB, :] = t
            for v in range(2):
                for d in range(3):
                    vals[side, h, v, d] = held[v, pl.ds(tile.column(side, d), 16, stride=SUB), :]
    for h in range(2):
        lane = slice(h * LANES, (h + 1) * LANES)
        for v in range(2):
            for d in range(3):
                west, east = vals[0, h, v, d], vals[1, h, v, d]
                at = slice(d * 16, d * 16 + 16)
                outs[v][at, lane] = jnp.where(first, west, east).astype(BF16)
                outs[2 + v][at, lane] = jnp.where(first, east, west).astype(BF16)


def unpack_columns(first, turn_near, turn_far, got):
    def value(side, h, d):
        lane = slice(h * LANES, (h + 1) * LANES)
        parts = [g[d * 16 : d * 16 + 16, lane].astype(F32) for g in got]
        one = jnp.where(turn_near, parts[1], parts[0])
        two = jnp.where(turn_far, parts[3], parts[2])
        return jnp.where(first, one, two) if side == 0 else jnp.where(first, two, one)

    return value


def ends_kernel(band, within, across, columns):
    rows, cols, _ = band.shape
    even = (lax.axis_index("tile") & 1) == 0
    for k in range(3):
        top, bottom = band[k], band[rows - 3 + k]
        within[k] = jnp.where(even, bottom, top)
        across[k] = jnp.where(even, top, bottom)
    for r in range(rows):
        columns[r, 0:16, :] = band[r, 0:16, :]
        columns[r, 16:32, :] = band[r, cols - 16 : cols, :]


def edges_kernel(columns, within, across, match, *refs):
    outs, flags, held = refs[:4], refs[4], refs[5]
    gluing(match, flags)
    up, down = above_below(within, across)
    rows, _, _ = columns.shape
    _, cols, _ = within.shape
    first, _, _ = glued(flags)

    def tile(side, h, i):
        lane = slice(h * LANES, (h + 1) * LANES)
        at = slice(0, 16) if side == 0 else slice(cols - 16, cols)
        if i < 3:
            v = up(i, at, lane)
        elif i < rows + 3:
            v = columns[i - 3, slice(0, 16) if side == 0 else slice(16, 32), lane]
        else:
            v = down(i - rows - 3, at, lane)
        return v.astype(F32)[0:SUB] if side == 0 else v.astype(F32)[SUB:16]

    tile.column = lambda side, d: d if side == 0 else SUB - 1 - d
    pack_columns(tile, rows + 6, first, held, outs)


def fill_pad(pad, halves, ext, wide, cols, source, which):
    for h in range(halves):
        lane = slice(h * LANES, (h + 1) * LANES)
        for i in which:
            at = (h * ext + i) * wide
            pad[at : at + LEAD, :] = jnp.zeros((LEAD, LANES), F32)
            pad[at + LEAD : at + LEAD + cols, :] = source(i, lane).astype(F32)
            pad[at + LEAD + cols : at + wide, :] = jnp.zeros((LEAD + SUB, LANES), F32)


def own_rows_kernel(band, kernel, bias, conv, taps, pad):
    for h in range(2):
        lane = slice(h * LANES, (h + 1) * LANES)
        for a in range(7):
            row = kernel[a].astype(F32)
            for b in range(7):
                taps[h, a * 7 + b] = jnp.broadcast_to(row[b : b + 1, lane], (SUB, LANES))
        taps[h, 49] = jnp.broadcast_to(bias[:, lane], (SUB, LANES))
    rows, cols, channels = band.shape
    halves = channels // LANES
    pitch = cols + 2 * LEAD
    wide = pitch + SUB
    ext = rows + 6
    groups = cols // SUB + 1
    cpitch = groups * SUB
    fill_pad(pad, halves, ext, wide, cols, lambda i, lane: band[i - 3, :, lane], range(3, rows + 3))

    def half(h, carry):
        for r in range(rows):
            acc = [taps[h, 49]] * groups
            for a in range(7):
                if not 3 <= r + a < rows + 3:
                    continue
                base = (h * ext + r + a) * wide + LEAD - 3
                tap = [taps[h, a * 7 + b] for b in range(7)]
                for jj in range(groups + 6):
                    x = strided(pad, base + jj, groups)
                    for b in range(7):
                        if 0 <= jj - b < groups:
                            acc[jj - b] = acc[jj - b] + tap[b] * x
            for j in range(groups):
                conv[pl.ds((h * rows + r) * cpitch + j, SUB, stride=groups), :] = acc[j]
        return carry

    lax.fori_loop(0, halves, half, 0)


def forward_kernel(
    band, within, across, got0, got1, got2, got3, cot, taps, gain, shift, bias2, scale, bias1, w1, w2, part, flags,
    result_out, pad_out, grad_out, mine, other, plain_near, plain_far, vecs, bias_out,
    result, pad, grad, conv, normed, act, pre, gbr, tmp, strip, sems,
):
    rows, cols, channels = band.shape
    halves = channels // LANES
    pitch = cols + 2 * LEAD
    wide = pitch + SUB
    ext = rows + 6
    groups = cols // SUB + 1
    cpitch = groups * SUB
    hidden = w1.shape[1]

    first, turn_near, turn_far = glued(flags)
    arrived = unpack_columns(first, turn_near, turn_far, (got0, got1, got2, got3))

    up, down = above_below(within, across)

    def source(i, lane):
        if i < 3:
            return up(i, slice(None), lane)
        return band[i - 3, :, lane] if i < rows + 3 else down(i - rows - 3, slice(None), lane)

    fill_pad(pad, halves, ext, wide, cols, source, range(ext))
    for h in range(halves):
        for d in range(3):
            for side in range(2):
                col = LEAD - 1 - d if side == 0 else LEAD + cols + d
                v = arrived(side, h, d)
                at = h * ext * wide + col
                pad[pl.ds(at, SUB, stride=wide), :] = v[0:SUB]
                pad[pl.ds(at + SUB * wide, ext - SUB, stride=wide), :] = v[SUB:ext]
        for r in range(rows):
            at = (h * rows + r) * pitch
            grad[at : at + LEAD, :] = jnp.zeros((LEAD, LANES), F32)
            grad[at + LEAD + cols : at + pitch, :] = jnp.zeros((LEAD, LANES), F32)

    keep_pad = pltpu.make_async_copy(pad, pad_out, sems.at[0])
    keep_pad.start()
    tail = halves * rows * pitch
    grad[tail : tail + SUB, :] = jnp.zeros((SUB, LANES), F32)

    where = lax.broadcasted_iota(jnp.int32, (SUB, LANES), 0)
    at_west, at_east = where == 0, where == SUB - 1
    none = jnp.zeros((SUB, LANES), F32)
    over = cols + 3 - (SUB - 1) * groups

    def complete(h, carry):
        for r in range(rows):
            acc = [strided(part, (h * rows + r) * cpitch + j, groups) for j in range(groups)]
            for a in range(7):
                base = (h * ext + r + a) * wide + LEAD - 3
                tap = [taps[h, a * 7 + b] for b in range(7)]
                if not 3 <= r + a < rows + 3:
                    for jj in range(groups + 6):
                        x = strided(pad, base + jj, groups)
                        for b in range(7):
                            if 0 <= jj - b < groups:
                                acc[jj - b] = acc[jj - b] + tap[b] * x
                    continue
                for d in range(3):
                    x = jnp.where(at_west, strided(pad, base + d, groups), none)
                    for b in range(d + 1):
                        acc[d - b] = acc[d - b] + tap[b] * x
                    x = jnp.where(at_east, strided(pad, base + over + d, groups), none)
                    for b in range(4 + d, 7):
                        acc[over + d - b] = acc[over + d - b] + tap[b] * x
            for j in range(groups):
                conv[pl.ds((h * rows + r) * cpitch + j, SUB, stride=groups), :] = acc[j]
        return carry

    lax.fori_loop(0, halves, complete, 0)

    step = 2 * cols
    gain, shift, bias2, scale = gain[...], shift[...], bias2[...], scale[...]
    tiles = hidden // 256

    def chunk(m, carry):
        s_conv, s_gain, s_norm, s_cot, s_scale = carry
        at = pl.multiple_of(m * step, step)
        x = jnp.concatenate(
            [
                jnp.concatenate(
                    [
                        conv[pl.ds(pl.multiple_of((h * rows + 2 * m + k) * cpitch, 8), cols), :]
                        for k in range(2)
                    ],
                    axis=0,
                )
                for h in range(halves)
            ],
            axis=1,
        )
        centred = x - jnp.mean(x, axis=-1, keepdims=True)
        inverse = lax.rsqrt(jnp.mean(centred * centred, axis=-1, keepdims=True) + EPSILON)
        standard = centred * inverse
        lane_in = (standard * gain + shift).astype(BF16)
        normed[pl.ds(at, step), :] = lane_in
        tmp[...] = standard
        upstream = cot[pl.ds(2 * m, 2)].reshape(step, channels).astype(F32)
        g_branch = (upstream * scale).astype(BF16)
        gbr[pl.ds(at, step), :] = g_branch
        for n in range(tiles):
            hid = slice(n * 256, (n + 1) * 256)
            v = dot(lane_in, w1[:, hid], ((1,), (0,))) + bias1[:, hid]
            v2 = v * v
            half = 0.5 + 0.5 * jnp.tanh(v * (ROOT_COEF + ROOT_COEF * CUBIC_COEF * v2))
            act[pl.ds(at, step), hid] = (v * half).astype(BF16)
            slope = half * (
                1.0 + (1.0 - half) * (v * (2 * ROOT_COEF + 6 * ROOT_COEF * CUBIC_COEF * v2))
            )
            d_act = dot(g_branch, w2[hid, :], ((1,), (1,)))
            g_pre = d_act * slope
            pre[pl.ds(at, step), hid] = g_pre.astype(BF16)
            bias_out[:, hid] += jnp.sum(g_pre, axis=0, keepdims=True)
        branch = dot(act[pl.ds(at, step), :], w2[...], ((1,), (0,))) + bias2
        residual = band[pl.ds(2 * m, 2)].reshape(step, channels).astype(F32)
        result[pl.ds(2 * m, 2)] = (
            (residual + scale * branch).astype(BF16).reshape(2, cols, channels)
        )
        s_cot = s_cot + jnp.sum(upstream, axis=0, keepdims=True)
        s_scale = s_scale + jnp.sum(upstream * branch, axis=0, keepdims=True)
        g_norm = dot(pre[pl.ds(at, step), :], w1[...], ((1,), (1,)))
        standard = tmp[...]
        u = g_norm * gain
        g_conv = (
            u
            - jnp.mean(u, axis=-1, keepdims=True)
            - standard * jnp.mean(u * standard, axis=-1, keepdims=True)
        ) * inverse
        for h in range(halves):
            for k in range(2):
                dst = (h * rows + 2 * m + k) * pitch + LEAD
                grad[pl.ds(pl.multiple_of(dst, 8), cols), :] = g_conv[
                    k * cols : (k + 1) * cols, h * LANES : (h + 1) * LANES
                ]
        s_conv = s_conv + jnp.sum(g_conv, axis=0, keepdims=True)
        s_gain = s_gain + jnp.sum(g_norm * standard, axis=0, keepdims=True)
        s_norm = s_norm + jnp.sum(g_norm, axis=0, keepdims=True)
        return (s_conv, s_gain, s_norm, s_cot, s_scale)

    bias_out[...] = jnp.zeros_like(bias_out)
    zero = jnp.zeros((1, channels), F32)
    sums = lax.fori_loop(0, rows // 2, chunk, (zero,) * 5, unroll=True)
    sums = (sums[0], sums[1], sums[2], sums[3] * scale, sums[4])
    vecs[...] = jnp.concatenate(list(sums) + [zero] * 3, axis=0)

    keep_grad = pltpu.make_async_copy(grad, grad_out, sems.at[1])
    keep_grad.start()
    keep_result = pltpu.make_async_copy(result, result_out, sems.at[2])
    keep_result.start()

    strip[...] = jnp.zeros_like(strip)
    for h in range(halves):
        lane = slice(h * LANES, (h + 1) * LANES)

        def column(c, h=h):
            return grad[pl.ds(h * rows * pitch + LEAD + c, SUB, stride=pitch), :]

        for side in range(2):
            edge = [column(c if side == 0 else cols - 1 - c) for c in range(3)]
            for d in range(3):
                slot = ((side * 3 + d) * halves + h) * 32
                for a in range(7):
                    total = none
                    for c in range(3 - d):
                        b = 2 - d - c if side == 0 else 4 + d + c
                        total = total + taps[h, a * 7 + b] * edge[c]
                    strip[slot + a : slot + a + SUB, :] += total
                for o in range(ext):
                    strip[slot + 16 + o : slot + 17 + o, :] = strip[
                        slot + ext - 1 - o : slot + ext - o, :
                    ]
        for d in range(3):
            slots = [((side * 3 + d) * halves + h) * 32 for side in range(2)]
            for turned in range(2):
                west, east = [strip[k + 16 * turned : k + 16 * turned + 16, :] for k in slots]
                one = jnp.where(first, west, east).astype(BF16)
                two = jnp.where(first, east, west).astype(BF16)
                if turned:
                    other[hidden + 16 * d : hidden + 16 * d + 16, lane] = one
                    other[hidden + 48 + 16 * d : hidden + 64 + 16 * d, lane] = two
                else:
                    plain_near[16 * d : 16 * d + 16, lane] = one
                    plain_far[16 * d : 16 * d + 16, lane] = two

    even = (lax.axis_index("tile") & 1) == 0
    for n in range(tiles):
        hid = slice(n * 256, (n + 1) * 256)
        g_expand = dot(normed[...], pre[:, hid], ((0,), (0,)))
        g_reduce = dot(act[:, hid], gbr[...], ((0,), (0,)))
        mine[hid, :] = jnp.where(even, g_expand, g_reduce)
        other[hid, :] = jnp.where(even, g_reduce, g_expand).astype(BF16)
    keep_pad.wait()
    keep_grad.wait()
    keep_result.wait()


def spread_row(grad, taps, h, o, rows, pitch, groups):
    acc = [jnp.zeros((SUB, LANES), F32)] * groups
    for a in range(7):
        if not 0 <= o - a < rows:
            continue
        src = (h * rows + o - a) * pitch + LEAD + 3
        tap = [taps[h, a * 7 + b] for b in range(7)]
        for jj in range(-6, groups):
            x = strided(grad, src + jj, groups)
            for b in range(7):
                if 0 <= jj + b < groups:
                    acc[jj + b] = acc[jj + b] + tap[b] * x
    return acc


def inner_kernel(h, grad, taps, out, token):
    token[...] = jnp.zeros_like(token)
    rows = 8
    cpitch = out.shape[0] // rows
    pitch = cpitch + LEAD
    groups = cpitch // SUB
    for r in range(rows):
        acc = spread_row(grad, taps, h, r + 3, rows, pitch, groups)
        for j in range(groups):
            out[pl.ds(r * cpitch + j, SUB, stride=groups), :] = acc[j]


def taps_kernel(h, grad, pad, out, token):
    token[...] = jnp.zeros_like(token)
    halves, rows = 2, 8
    ext = rows + 6
    pitch = (grad.shape[0] - SUB) // (halves * rows)
    wide = pad.shape[0] // (halves * ext)
    cols = pitch - 2 * LEAD
    groups = cols // SUB + 1

    def some(first, count):
        acc = [[jnp.zeros((SUB, LANES), F32)] * 7 for _ in range(count)]
        for i in range(rows + count - 1):
            base = (h * ext + i + first) * wide + LEAD - 3
            use = [k for k in range(count) if 0 <= i - k < rows]
            g = {}
            for jj in range(groups + 6):
                if jj < groups:
                    for k in use:
                        at = (h * rows + i - k) * pitch + LEAD + jj
                        g[k, jj] = strided(grad, at, groups)
                x = strided(pad, base + jj, groups)
                for b in range(7):
                    j = jj - b
                    if 0 <= j < groups:
                        for k in use:
                            acc[k][b] = acc[k][b] + g[k, j] * x
        for k in range(count):
            for b in range(7):
                out[pl.ds((first + k) * 7 + b, 1), :] = jnp.sum(acc[k][b], axis=0, keepdims=True)

    def pair(p, carry):
        some(2 * p, 2)
        return carry

    lax.fori_loop(0, 3, pair, 0)
    some(6, 1)


def rims_kernel(grad, taps, got0, got1, got2, got3, flags, within, across, token, total, held):
    token[...] = jnp.zeros_like(token)
    halves, _, cols, _ = within.shape
    even = (lax.axis_index("tile") & 1) == 0
    rows = 8
    pitch = cols + 2 * LEAD
    groups = cols // SUB + 1
    cpitch = groups * SUB
    first, turn_near, turn_far = glued(flags)
    arrived = unpack_columns(first, turn_near, turn_far, (got0, got1, got2, got3))
    for h in range(halves):
        for k in range(6):
            acc = spread_row(grad, taps, h, k if k < 3 else rows + k, rows, pitch, groups)
            for j in range(groups):
                total[pl.ds(k * cpitch + j, SUB, stride=groups), :] = acc[j]
        for side in range(2):
            for d in range(3):
                held[...] = arrived(side, h, d)
                for k in range(6):
                    o = k if k < 3 else k + 8
                    at = k * cpitch + (d if side == 0 else cols - 1 - d)
                    total[at : at + 1, :] += held[o : o + 1, :]
        for k in range(3):
            top = total[k * cpitch : k * cpitch + cols, :].astype(BF16)
            bottom = total[(k + 3) * cpitch : (k + 3) * cpitch + cols, :].astype(BF16)
            within[h, k] = jnp.where(even, bottom, top)
            across[h, k] = jnp.where(even, top, bottom)


def fields_kernel(inner0, inner1, within, across, got0, got1, got2, got3, cot, flags, out, token, total, held):
    token[...] = jnp.zeros_like(token)
    rows, cols, channels = cot.shape
    halves = channels // LANES
    cpitch = inner0.shape[0] // rows
    from_up, from_down = above_below(within, across)
    first, turn_near, turn_far = glued(flags)
    arrived = unpack_columns(first, turn_near, turn_far, (got0, got1, got2, got3))
    for h in range(halves):
        lane = slice(h * LANES, (h + 1) * LANES)
        for r in range(rows):
            at = r * cpitch
            own = (inner0, inner1)[h][at : at + cols, :] + cot[r, :, lane].astype(F32)
            if r < 3:
                own = own + from_up(h, r).astype(F32)
            if r >= rows - 3:
                own = own + from_down(h, r - rows + 3).astype(F32)
            total[r * cols : (r + 1) * cols, :] = own
        for side in range(2):
            for d in range(3):
                held[...] = arrived(side, h, d)
                at = pl.ds(d if side == 0 else cols - 1 - d, SUB, stride=cols)
                total[at, :] = total[at, :] + held[3 : 3 + rows, :]
        for r in range(rows):
            out[r, :, lane] = total[r * cols : (r + 1) * cols, :].astype(BF16)


def merge_kernel(masks, half, mine, peer, plain_near, plain_far, flags, own, token, *messages):
    _, turn_near, turn_far = glued(flags)
    token[...] = jnp.zeros_like(token)
    hidden = mine.shape[0]
    count = own.shape[0]
    face = lax.axis_index("face")

    def share(mask):
        at = pl.ds(pl.multiple_of((face ^ mask) * count, count), count)
        return mine[at, :] + peer[at, :].astype(F32)

    def choose(turn, at, plain, message):
        for h in range(2):
            lane = slice(h * LANES, (h + 1) * LANES)
            turned = peer[at : at + 48, lane].astype(F32)
            message[count : count + 48, lane] = jnp.where(
                turn, turned, plain[:, lane].astype(F32)
            ).astype(BF16)

    own[...] = share(0)
    for mask, message in zip(masks, messages):
        message[0:count, :] = share(mask).astype(BF16)
        if mask == 1:
            choose(turn_near, hidden, plain_near, message)
        if mask == half:
            choose(turn_far, hidden + 48, plain_far, message)


def deal_kernel(masks, mirror, near, far, own, *refs):
    count = own.shape[0]
    got, (part, token, *messages), total = refs[: len(refs) - 3 - len(masks)], refs[
        len(refs) - 3 - len(masks) : -1
    ], refs[-1]
    token[...] = jnp.zeros_like(token)
    size = part.shape[0]
    chip = lax.axis_index("tile") >> 1
    total[...] = tree_sum([own[...]] + [g[0:count, :] for g in got])

    def share(place):
        return total[pl.ds(pl.multiple_of(place * size, size), size), :]

    part[...] = share(chip)
    for mask, message in zip(masks, messages):
        at = 0
        if mask == mirror:
            message[0:48, :] = got[near][count:, :]
            message[48:96, :] = got[far][count:, :]
            at = 96
        message[at : at + size, :] = share(chip ^ (mask >> 1)).astype(BF16)


def pack_shares_kernel(own, *refs):
    *got, taps0, taps1, bias, vecs, out, held = refs
    count, channels = own.shape
    held[...] = jnp.zeros_like(held)
    held[0:49, 0:LANES] = taps0[0:49, :]
    held[0:49, LANES : 2 * LANES] = taps1[0:49, :]
    parts = bias.shape[1] // channels
    for n in range(parts):
        held[49 + n : 50 + n, :] = bias[:, n * channels : (n + 1) * channels]
    held[49 + parts : 54 + parts, :] = vecs[0:5, :]
    out[0:SMALL, :] = held[...].astype(BF16)
    out[SMALL:, :] = tree_sum([own[...]] + [g[0:count, :] for g in got]).astype(BF16)


def pack_pieces_kernel(own, *refs):
    *got, out = refs
    parts = [own[...].astype(F32)] + [g[...].astype(F32) for g in got]
    out[0:SMALL, :] = tree_sum([p[0:SMALL] for p in parts]).astype(BF16)
    out[SMALL:, :] = jnp.concatenate([p[SMALL:] for p in parts], 0).astype(BF16)


def finish_kernel(factor, faces, chips, mine, peer, expand, reduce, g_taps, g_bias, vecs):
    hidden, channels = reduce.shape
    count = hidden // (faces * chips)
    face = lax.axis_index("face")
    chip = lax.axis_index("tile") >> 1
    even = (lax.axis_index("tile") & 1) == 0
    small = mine[0:SMALL, :].astype(F32) + peer[0:SMALL, :].astype(F32)
    small = small * factor
    for f in range(faces):
        for z in range(chips):
            at = SMALL + (f * chips + z) * count
            own = mine[at : at + count, :].astype(F32) * factor
            got = peer[at : at + count, :].astype(F32) * factor
            to = ((face ^ f) * chips + (chip ^ z)) * count
            reduce[pl.ds(pl.multiple_of(to, count), count), :] = jnp.where(even, got, own)
            row = pl.multiple_of(lax.rem(to, channels), count)
            col = pl.multiple_of((to // channels) * channels, channels)
            expand[pl.ds(row, count), pl.ds(col, channels)] = jnp.where(even, own, got)
    for a in range(7):
        g_taps[a] = small[a * 7 : a * 7 + 7, :]
    for n in range(hidden // channels):
        g_bias[:, n * channels : (n + 1) * channels] = small[49 + n : 50 + n, :]
    first = 49 + hidden // channels
    vecs[...] = small[first : first + 5, :]


def face_swap(x, mask, turned=False):
    faces, tiles = lax.axis_size("face"), lax.axis_size("tile")
    pairs = [
        (f * tiles + t, (f ^ mask) * tiles + (tiles - 1 - t if turned else t))
        for f in range(faces)
        for t in range(tiles)
    ]
    return lax.ppermute(x, ("face", "tile"), pairs)


def glued_swap(strips):
    near_plain, near_turned, far_plain, far_turned = strips
    half = lax.axis_size("face") // 2
    return (
        face_swap(near_plain, 1),
        face_swap(near_turned, 1, True),
        face_swap(far_plain, half),
        face_swap(far_turned, half, True),
    )


def row_swap(within, across):
    count = lax.axis_size("tile")
    pairs = [(i, i + 1) for i in range(1, count - 1, 2)]
    return (
        swapped(within, "tile", 1),
        lax.ppermute(across, "tile", pairs + [(j, i) for i, j in pairs]),
    )


def above_below(within, across):
    even = (lax.axis_index("tile") & 1) == 0

    def up(*at):
        return jnp.where(even, across[at], within[at])

    def down(*at):
        return jnp.where(even, within[at], across[at])

    return up, down


def swapped(x, axis, mask):
    return lax.ppermute(x, axis, [(i, i ^ mask) for i in range(lax.axis_size(axis))])


def tree_sum(parts):
    parts = [p.astype(F32) for p in parts]
    while len(parts) > 1:
        parts = [parts[i] + parts[i + 1] for i in range(0, len(parts), 2)]
    return parts[0]


def gathered(x, axis, masks):
    got = [swapped(x, axis, m) for m in masks]
    return [x] + [got[masks.index(m)] for m in sorted(masks)]


def shards(
    fields,
    cotangent,
    edge_match,
    depth_kernel,
    depth_bias,
    norm_gain,
    norm_bias,
    expand_weight,
    expand_bias,
    reduce_weight,
    reduce_bias,
    layer_scale,
):
    band = fields[0]
    cot = cotangent[0]
    rows, cols, channels = band.shape
    halves = channels // LANES
    hidden = expand_weight.shape[1]
    pitch = cols + 2 * LEAD
    wide = pitch + SUB
    ext = rows + 6
    cells = rows * cols
    faces, tiles = lax.axis_size("face"), lax.axis_size("tile")
    shape = jax.ShapeDtypeStruct
    strips = [shape((48, channels), BF16)] * 4
    sign = shape((SUB, LANES), F32)

    *rim_rows, columns = call(
        ends_kernel,
        [
            shape((3, cols, channels), BF16),
            shape((3, cols, channels), BF16),
            shape((rows, 32, channels), BF16),
        ],
        [],
        1_000_000_000,
        (band,),
    )
    beside = row_swap(*rim_rows)
    *sides, flags = call(
        edges_kernel,
        strips + [sign],
        [pltpu.VMEM((2, 16 * SUB, LANES), F32)],
        900_000_000,
        (columns, *beside, edge_match),
        smem=1,
    )
    got = glued_swap(sides)
    part, taps = call(
        own_rows_kernel,
        [
            pltpu.VMEM((halves * rows * (cols + SUB), LANES), F32),
            pltpu.VMEM((halves, 50, SUB, LANES), F32),
        ],
        [pltpu.VMEM((halves * ext * wide, LANES), F32)],
        4_500_000_000,
        (band, depth_kernel, depth_bias[None]),
        limit=4,
        after=(sides[0],),
    )
    part, taps = kept(part), kept(taps)
    result, pad, grad, mine, other, plain_near, plain_far, vecs, bias_out = call(
        forward_kernel,
        [
            pltpu.HBM(band.shape, BF16),
            pltpu.HBM((halves * ext * wide, LANES), F32),
            pltpu.HBM((halves * rows * pitch + SUB, LANES), F32),
            shape((hidden, channels), F32),
            shape((hidden + 96, channels), BF16),
            shape((48, channels), BF16),
            shape((48, channels), BF16),
            shape((8, channels), F32),
            shape((1, hidden), F32),
        ],
        [
            pltpu.VMEM(band.shape, BF16),
            pltpu.VMEM((halves * ext * wide, LANES), F32),
            pltpu.VMEM((halves * rows * pitch + SUB, LANES), F32),
            pltpu.VMEM((halves * rows * (cols + SUB), LANES), F32),
            pltpu.VMEM((cells, channels), BF16),
            pltpu.VMEM((cells, hidden), BF16),
            pltpu.VMEM((cells, hidden), BF16),
            pltpu.VMEM((cells, channels), BF16),
            pltpu.VMEM((2 * cols, channels), F32),
            pltpu.VMEM((12 * 32, LANES), F32),
            pltpu.SemaphoreType.DMA((3,)),
        ],
        12_000_000_000,
        (
            band, *beside, *got, cot, taps, norm_gain[None], norm_bias[None], reduce_bias[None],
            layer_scale[None], expand_bias.reshape(1, hidden), expand_weight, reduce_weight, part,
            flags,
        ),
        limit=20,
        left=(0, 1, 2),
    )

    face_masks = list(range(faces - 1, 0, -1))
    chip_masks = list(range(tiles - 2, 0, -2))
    half, mirror = faces // 2, tiles - 2
    peer = swapped(other, "tile", 1)
    count = hidden // faces
    own, merged, *messages = call(
        lambda *refs: merge_kernel(face_masks, half, *refs),
        [shape((count, channels), F32), sign]
        + [shape((count + 48 * (m in (1, half)), channels), BF16) for m in face_masks],
        [],
        500_000_000,
        (mine, peer, plain_near, plain_far, flags),
    )

    def half_taps(h, after):
        return call(
            lambda *refs: taps_kernel(h, *refs),
            [shape((56, LANES), F32), sign],
            [],
            3_500_000_000 if h == 0 else 300_000_000,
            (grad, pad),
            after=after,
        )

    def half_inner(h, after):
        return call(
            lambda *refs: inner_kernel(h, *refs),
            [shape((rows * (cols + SUB), LANES), F32), sign],
            [],
            2_100_000_000 if h == 0 else 200_000_000,
            (grad, taps),
            after=after,
        )

    got = [swapped(v, "face", m) for v, m in zip(messages, face_masks)]
    rode = {m: got[face_masks.index(m)][count:] for m in (1, half)}
    inner0, token = half_inner(0, (merged,))
    taps0, token = half_taps(0, (token,))
    rows_z, rows_f = hidden // (faces * (tiles // 2)), hidden // faces
    got = got[::-1]
    part, dealt, *messages = call(
        lambda *refs: deal_kernel(chip_masks, mirror, 0, half - 1, *refs),
        [shape((rows_z, channels), F32), sign]
        + [shape((rows_z + 96 * (m == mirror), channels), BF16) for m in chip_masks],
        [pltpu.VMEM((rows_f, channels), F32)],
        100_000_000,
        (own, *got),
        after=(token,),
    )
    straight = rode
    got = [swapped(v, "tile", m) for v, m in zip(messages, chip_masks)]
    strips_got = got[chip_masks.index(mirror)]
    got = [g[96:] if m == mirror else g for g, m in zip(got, chip_masks)]
    columns = (straight[1], strips_got[0:48], straight[half], strips_got[48:96])
    taps1, _ = half_taps(1, (dealt,))
    (share,) = call(
        pack_shares_kernel,
        [shape((SMALL + rows_z, channels), BF16)],
        [pltpu.VMEM((SMALL, channels), F32)],
        1_000_000,
        (part, *got, taps0, taps1, bias_out, vecs),
    )
    got = gathered(share, "tile", chip_masks)
    within, across, token = call(
        rims_kernel,
        [shape((halves, 3, cols, LANES), BF16)] * 2 + [sign],
        [pltpu.VMEM((6 * (cols + SUB), LANES), F32), pltpu.VMEM((16, LANES), F32)],
        900_000_000,
        (grad, taps, *columns, flags),
    )
    arrived = row_swap(within, across)
    (pieces,) = call(
        pack_pieces_kernel,
        [shape((SMALL + rows_f, channels), BF16)],
        [],
        1_000_000,
        tuple(got),
        after=(token,),
    )
    got = gathered(pieces, "face", face_masks)
    inner1, _ = half_inner(1, (pieces,))
    grad_fields, token = call(
        fields_kernel,
        [shape(band.shape, BF16), sign],
        [pltpu.VMEM((cells, LANES), F32), pltpu.VMEM((16, LANES), F32)],
        200_000_000,
        (inner0, inner1, *arrived, *columns, cot, flags),
    )
    (pieces,) = call(
        pack_pieces_kernel,
        [shape((SMALL + hidden, channels), BF16)],
        [],
        1_000_000,
        tuple(got),
        after=(token,),
    )
    peer = swapped(pieces, "tile", 1)

    factor = 1.0 / math.sqrt(faces * tiles * cells)

    def finish(*refs):
        finish_kernel(factor, faces, tiles // 2, *refs)

    g_expand, g_reduce, g_taps, g_bias, g_vecs = call(
        finish,
        [
            shape((channels, hidden), F32),
            shape((hidden, channels), F32),
            shape((7, 7, channels), F32),
            shape((1, hidden), F32),
            shape((5, channels), F32),
        ],
        [],
        2_000_000_000,
        (pieces, peer),
    )
    return (
        result[None],
        grad_fields[None],
        g_taps,
        g_expand,
        g_reduce,
        g_bias.reshape(hidden),
        g_vecs,
    )


def solution(mesh):
    return jax.shard_map(
        shards,
        mesh=mesh,
        in_specs=(P("face", "tile"), P("face", "tile")) + (P(),) * 10,
        out_specs=(P("face", "tile"), P("face", "tile")) + (P(),) * 5,
        check_vma=False,
    )
```
